32 devices in a mesh: dp: 8 (over z, x), mp: 4 (over y, core).
Axes of the slice: x: 2, y: 2, z: 4, core: 2. Of those that a mesh axis runs over, the one named last changes fastest.
Arguments:
- image_embed: bfloat16 [4096, 1152], P(('dp', 'mp')), may hold values from -0.176776695 to 0.176776695
- text_embed: bfloat16 [4096, 1152], P(('dp', 'mp')), may hold values from -0.176776695 to 0.176776695
- log_scale: float32 [1], replicated, may hold values from 1.1 to 2.3
- logit_bias: float32 [1], replicated, may hold values from -3 to -1
Outputs:
- loss: float32 [1], replicated
- image_grad: float32 [4096, 1152], P(('dp', 'mp'))
- text_grad: float32 [4096, 1152], P(('dp', 'mp'))
The draws below stay inside these ranges and needn't reach their ends.
All inputs are finite; a program needn't handle non-finite values.
Results may differ from the reference program's by a relative error of at most 0.0015.
Values may be sent and summed in bfloat16 or wider, within the bound.
A program may use at most 128 MiB of HBM per device.

```python
import jax
import jax.numpy as jnp
from jax import lax

D = 1152
STEPS = 2
GROUP = 512
BATCH = 4096
N_DP = 8


def shared_direction(key):
    direction = jax.random.normal(key, (D,), jnp.float32)
    return direction / jnp.sqrt(jnp.sum(direction * direction))


def build_rows(key, base, power, start, reach):
    position = jnp.arange(BATCH, dtype=jnp.float32) / BATCH
    weight = start + reach * position ** power
    noise = jax.random.normal(key, (BATCH, D), jnp.float32)
    noise = noise * D ** (-0.5)
    rows = weight[:, None] * base[None, :] + jnp.sqrt(1.0 - weight * weight)[:, None] * noise
    limit = 6.0 * D ** (-0.5)
    return jnp.clip(rows, -limit, limit).astype(jnp.bfloat16)


def draw_image_embed(key, part):
    base = shared_direction(key)
    key = jax.random.fold_in(key, 11)
    return build_rows(key, base, 1.0, 0.1, 0.85)


def draw_text_embed(key, part):
    base = shared_direction(key)
    key = jax.random.fold_in(key, 23)
    return build_rows(key, base, 1.0, 0.1, 0.85)


def setup_inputs(seed: int = 0) -> dict:
    keys = jax.random.split(jax.random.key(seed), 5)
    return {
        "image_embed": draw_image_embed(jax.random.fold_in(keys[4], 71), 0),
        "text_embed": draw_text_embed(jax.random.fold_in(keys[4], 71), 0),
        "log_scale": jnp.clip(jax.random.uniform(keys[2], (1,), jnp.float32, 1.1, 2.3), 1.1, 2.3),
        "logit_bias": jnp.clip(jax.random.uniform(keys[3], (1,), jnp.float32, -3.0, -1.0), -3.0, -1.0),
    }


def unit_rows(raw):
    values = raw.astype(jnp.float32)
    norm = jnp.sqrt(lax.optimization_barrier(jnp.sum(values * values, axis=1, keepdims=True)) + 1e-06)
    unit = values / norm
    return (unit, unit.astype(jnp.bfloat16), norm)

def back_norm(hat, unit, norm):
    return (hat - unit * lax.optimization_barrier(jnp.sum(unit * hat, axis=1, keepdims=True))) / norm

def reference(image_embed, text_embed, log_scale, logit_bias):
    image_unit, image_low, image_norm = unit_rows(image_embed)
    text_unit, text_low, text_norm = unit_rows(text_embed)
    scale = jnp.exp(log_scale[0])
    bias = logit_bias[0]
    image_hat = jnp.zeros((BATCH, D), jnp.float32)
    text_hat = jnp.zeros((BATCH, D), jnp.float32)
    total = jnp.zeros((), jnp.float32)
    for group in range(N_DP):
        image_part = image_low[group * GROUP:(group + 1) * GROUP]
        for step in range(STEPS):
            other = (group - step) % N_DP
            text_part = text_low[other * GROUP:(other + 1) * GROUP]
            logits = scale * jnp.dot(image_part, text_part.T, preferred_element_type=jnp.float32) + bias
            if step == 0:
                label = 2.0 * jnp.eye(GROUP, dtype=jnp.float32) - 1.0
            else:
                label = -jnp.ones((GROUP, GROUP), jnp.float32)
            total = total + jnp.sum(jax.nn.softplus(-label * logits))
            coef = (-label * jax.nn.sigmoid(-label * logits)).astype(jnp.bfloat16)
            image_hat = image_hat.at[group * GROUP:(group + 1) * GROUP].add(jnp.dot(coef, text_part, preferred_element_type=jnp.float32))
            text_hat = text_hat.at[other * GROUP:(other + 1) * GROUP].add(jnp.dot(coef.T, image_part, preferred_element_type=jnp.float32))
    loss = jnp.reshape(total / (BATCH * STEPS * GROUP), (1,))
    image_grad = back_norm(scale * image_hat, image_unit, image_norm)
    text_grad = back_norm(scale * text_hat, text_unit, text_norm)
    return (loss, image_grad, text_grad)
```

```python
import functools

import jax
import jax.numpy as jnp
from jax import lax
from jax.experimental import pallas as pl
from jax.experimental.pallas import tpu as pltpu
from jax.sharding import PartitionSpec as P

STEPS = 2
MESH = pl.DeviceIdType.MESH
NT = (((1,), (1,)), ((), ()))


def unit_rows(raw):
    values = raw.astype(jnp.float32)
    norm = jnp.sqrt(jnp.sum(values * values, axis=1, keepdims=True) + 1e-06)
    return (values / norm, norm)


def back_norm(hat, raw):
    unit, norm = unit_rows(raw)
    return (hat - unit * jnp.sum(unit * hat, axis=1, keepdims=True)) / norm


def fold(values):
    rows, columns = values.shape
    tall = values[0:8]
    for r in range(8, rows, 8):
        tall = tall + values[r : r + 8]
    tile = tall[:, 0:128]
    for c in range(128, columns, 128):
        tile = tile + tall[:, c : c + 128]
    return tile


def kernel(
    n_dp, n_mp, image_ref, text_ref, log_scale_ref, bias_ref,
    loss_ref, image_grad_ref, text_grad_ref,
    texts, images, image_hat, text_hat, term_sum, group_terms, all_terms,
    send_sem, row_sem, group_sem, all_sem,
):
    rows, width = image_ref.shape
    chips = n_mp // 2
    g, m = lax.axis_index("dp"), lax.axis_index("mp")
    c, k = m // 2, lax.rem(m, 2)
    sibling = 2 * c + 1 - k
    after, before = lax.rem(g + 1, n_dp), lax.rem(g + n_dp - 1, n_dp)

    def same_core(d):
        return 2 * lax.rem(c + d, chips) + k

    def peer(d):
        return lax.rem(m + d, n_mp)

    def ring(d):
        return lax.rem(g + d, n_dp)

    partners = [(g, peer(d)) for d in range(1, n_mp)]
    partners += [(p, same_core(d)) for p in (after, before) for d in range(chips)]
    partners += [(ring(d), m) for d in range(2, n_dp - 1)]
    barrier = pltpu.get_barrier_semaphore()
    for partner in partners:
        pl.semaphore_signal(barrier, inc=1, device_id=partner, device_id_type=MESH)

    def block(ref, step, index):
        return ref.at[step, pl.ds(pl.multiple_of(index * rows, rows), rows), :]

    image_low = unit_rows(image_ref[...])[0].astype(jnp.bfloat16)
    text_low = unit_rows(text_ref[...])[0].astype(jnp.bfloat16)
    block(images, 0, m)[...] = image_low
    block(texts, 0, m)[...] = text_low
    pl.semaphore_wait(barrier, len(partners))

    sends = []

    def push(src, dst, recv, device):
        copy = pltpu.make_async_remote_copy(
            src_ref=src, dst_ref=dst, send_sem=send_sem.at[len(sends)], recv_sem=recv,
            device_id=device, device_id_type=MESH,
        )
        copy.start()
        sends.append(copy)

    def send_block(which, step, index, device, to_step=None):
        ref = (texts, images)[which]
        to_step = step if to_step is None else to_step
        push(block(ref, step, index), block(ref, to_step, index),
             row_sem.at[which, to_step, index], device)

    def take_block(which, step, index):
        ref = (texts, images)[which]
        pltpu.make_async_remote_copy(
            src_ref=block(ref, step, index), dst_ref=block(ref, step, index),
            send_sem=send_sem.at[0], recv_sem=row_sem.at[which, step, index],
            device_id=(g, sibling), device_id_type=MESH,
        ).wait_recv()

    for which in range(2):
        for d in range(1, chips):
            send_block(which, 0, m, (g, same_core(d)))
        send_block(which, 0, m, (g, sibling))
    for which, other in ((0, after), (1, before)):
        for d in range(chips):
            send_block(which, 0, m, (other, same_core(d)), 1)

    def forward(which, step):
        for d in range(1 if step == 0 else 0, chips):
            take_block(which, step, same_core(d))
            send_block(which, step, same_core(d), (g, sibling))

    def take_sibling(which, step):
        for d in range(chips):
            take_block(which, step, 2 * lax.rem(c + d, chips) + 1 - k)

    scale = jnp.exp(jnp.full((rows, 1), log_scale_ref[0], jnp.float32))
    bias = bias_ref[0]
    chunk = min(512, n_mp * rows)
    own = m * rows + lax.broadcasted_iota(jnp.int32, (rows, chunk), 0)

    def score(which, step):
        low = block((images, texts)[which], 0, m)
        ref = (texts, images)[which]
        hat = (image_hat, text_hat)[which]

        def part(n):
            start = n * chunk if isinstance(n, int) else pl.multiple_of(n * chunk, chunk)
            others = ref[step, pl.ds(start, chunk), :]
            z = scale * lax.dot_general(low[...], others, NT, preferred_element_type=jnp.float32) + bias
            if step == 0:
                column = start + lax.broadcasted_iota(jnp.int32, (rows, chunk), 1)
                x = jnp.where(own == column, -z, z)
            else:
                x = z
            e = jnp.exp(-jnp.abs(x))
            sigmoid = jnp.where(x >= 0, 1.0, e) / (1.0 + e)
            if step == 0:
                sigmoid = jnp.where(own == column, -sigmoid, sigmoid)
            update = jnp.dot(sigmoid.astype(jnp.bfloat16), others, preferred_element_type=jnp.float32)
            if step == 0 and isinstance(n, int) and n == 0:
                hat[...] = update
            else:
                hat[...] += update
            if which == 0:
                terms = fold(jnp.maximum(x, 0.0) + jnp.log1p(e))
                if step == 0 and isinstance(n, int) and n == 0:
                    term_sum[...] = terms
                else:
                    term_sum[...] += terms

        part(0)
        if n_mp * rows > chunk:
            @pl.loop(1, n_mp * rows // chunk)
            def _(n):
                part(n)

    forward(0, 0)
    forward(1, 0)
    take_sibling(0, 0)
    score(0, 0)
    take_sibling(1, 0)
    score(1, 0)
    forward(0, 1)
    forward(1, 1)
    take_sibling(0, 1)
    score(0, 1)

    group_terms[m] = term_sum[...]
    for d in range(1, n_mp):
        push(group_terms.at[m], group_terms.at[m], group_sem.at[m], (g, peer(d)))
    image_grad_ref[...] = back_norm(scale * image_hat[...], image_ref[...])
    take_sibling(1, 1)
    score(1, 1)
    for d in range(1, n_mp):
        pltpu.make_async_remote_copy(
            src_ref=group_terms.at[peer(d)], dst_ref=group_terms.at[peer(d)],
            send_sem=send_sem.at[0], recv_sem=group_sem.at[peer(d)],
            device_id=(g, sibling), device_id_type=MESH,
        ).wait_recv()
    all_terms[g] = jnp.sum(group_terms[...], axis=0)
    for d in range(1, n_dp):
        push(all_terms.at[g], all_terms.at[g], all_sem.at[g], (ring(d), m))
    text_grad_ref[...] = back_norm(scale * text_hat[...], text_ref[...])
    for d in range(1, n_dp):
        pltpu.make_async_remote_copy(
            src_ref=all_terms.at[ring(d)], dst_ref=all_terms.at[ring(d)],
            send_sem=send_sem.at[0], recv_sem=all_sem.at[ring(d)],
            device_id=(g, sibling), device_id_type=MESH,
        ).wait_recv()
    pair_count = n_dp * n_mp * rows * STEPS * n_mp * rows
    loss_ref[0] = jnp.sum(jnp.sum(all_terms[...], axis=0)) / pair_count
    for copy in sends:
        copy.wait_send()


def solution(mesh):
    n_dp, n_mp = mesh.shape["dp"], mesh.shape["mp"]

    def body(image_embed, text_embed, log_scale, logit_bias):
        rows, width = image_embed.shape
        chips = n_mp // 2
        n_sends = 2 * chips + 2 * chips + 2 * (2 * chips - 1) + (n_mp - 1) + (n_dp - 1)
        vmem = pl.BlockSpec(memory_space=pltpu.VMEM)
        smem = pl.BlockSpec(memory_space=pltpu.SMEM)
        grad = jax.ShapeDtypeStruct((rows, width), jnp.float32)
        return pl.pallas_call(
            functools.partial(kernel, n_dp, n_mp),
            out_shape=(jax.ShapeDtypeStruct((1,), jnp.float32), grad, grad),
            in_specs=[vmem, vmem, smem, smem],
            out_specs=(smem, vmem, vmem),
            scratch_shapes=[
                pltpu.VMEM((2, n_mp * rows, width), jnp.bfloat16),
                pltpu.VMEM((2, n_mp * rows, width), jnp.bfloat16),
                pltpu.VMEM((rows, width), jnp.float32),
                pltpu.VMEM((rows, width), jnp.float32),
                pltpu.VMEM((8, 128), jnp.float32),
                pltpu.VMEM((n_mp, 8, 128), jnp.float32),
                pltpu.VMEM((n_dp, 8, 128), jnp.float32),
                pltpu.SemaphoreType.DMA((n_sends,)),
                pltpu.SemaphoreType.DMA((2, 2, n_mp)),
                pltpu.SemaphoreType.DMA((n_mp,)),
                pltpu.SemaphoreType.DMA((n_dp,)),
            ],
            compiler_params=pltpu.CompilerParams(
                collective_id=0, has_side_effects=True, vmem_limit_bytes=40 * 1024 * 1024
            ),
        )(image_embed, text_embed, log_scale, logit_bias)

    rows_spec = P(("dp", "mp"), None)
    return jax.shard_map(
        body,
        mesh=mesh,
        in_specs=(rows_spec, rows_spec, P(), P()),
        out_specs=(P(), rows_spec, rows_spec),
        check_vma=False,
    )
```

```python
import functools

import jax
import jax.numpy as jnp
from jax import lax
from jax.experimental import pallas as pl
from jax.experimental.pallas import tpu as pltpu
from jax.sharding import PartitionSpec as P

STEPS = 2
MESH = pl.DeviceIdType.MESH
NT = (((1,), (1,)), ((), ()))


def unit_rows(raw):
    values = raw.astype(jnp.float32)
    norm = jnp.sqrt(jnp.sum(values * values, axis=1, keepdims=True) + 1e-06)
    return (values / norm, norm)


def back_norm(hat, raw):
    unit, norm = unit_rows(raw)
    return (hat - unit * jnp.sum(unit * hat, axis=1, keepdims=True)) / norm


def fold(values):
    rows, columns = values.shape
    tall = values[0:8]
    for r in range(8, rows, 8):
        tall = tall + values[r : r + 8]
    tile = tall[:, 0:128]
    for c in range(128, columns, 128):
        tile = tile + tall[:, c : c + 128]
    return tile


def kernel(
    n_dp, n_mp, image_hbm, text_hbm, log_scale_ref, bias_ref,
    loss_ref, image_grad_ref, text_grad_ref,
    image_ref, text_ref, texts, images, image_hat, text_hat, term_sum, group_terms, all_terms,
    load_sem, send_sem, row_sem, group_sem, all_sem,
):
    rows = image_ref.shape[0]
    chips, half = n_mp // 2, rows // 2
    g, m = lax.axis_index("dp"), lax.axis_index("mp")
    c, k = m // 2, lax.rem(m, 2)
    sibling = 2 * c + 1 - k
    towards = (lax.rem(g + 1, n_dp), lax.rem(g + n_dp - 1, n_dp))

    def same_core(d):
        return 2 * lax.rem(c + d, chips) + k

    def peer(d):
        return lax.rem(m + d, n_mp)

    def ring(d):
        return lax.rem(g + d, n_dp)

    loads = [
        pltpu.make_async_copy(text_hbm, text_ref, load_sem.at[0]),
        pltpu.make_async_copy(image_hbm, image_ref, load_sem.at[1]),
    ]
    for load in loads:
        load.start()

    partners = [(g, peer(d)) for d in range(1, n_mp)]
    partners += [(ring(d), m) for d in range(1, n_dp)]
    barrier = pltpu.get_barrier_semaphore()
    for partner in partners:
        pl.semaphore_signal(barrier, inc=1, device_id=partner, device_id_type=MESH)

    def block(which, step, index, part=None):
        ref = (texts, images)[which]
        if part is None:
            return ref.at[step, pl.ds(pl.multiple_of(index * rows, rows), rows), :]
        start = pl.multiple_of(index * rows + part * half, half)
        return ref.at[step, pl.ds(start, half), :]

    for which, ref in enumerate((text_ref, image_ref)):
        loads[which].wait()
        block(which, 0, m)[...] = unit_rows(ref[...])[0].astype(jnp.bfloat16)
    pl.semaphore_wait(barrier, len(partners))

    sends = []

    def push(src, dst, recv, device):
        copy = pltpu.make_async_remote_copy(
            src_ref=src, dst_ref=dst, send_sem=send_sem.at[len(sends)], recv_sem=recv,
            device_id=device, device_id_type=MESH,
        )
        copy.start()
        sends.append(copy)

    def await_copy(dst, recv):
        pltpu.make_async_remote_copy(
            src_ref=dst, dst_ref=dst, send_sem=send_sem.at[0], recv_sem=recv,
            device_id=(g, sibling), device_id_type=MESH,
        ).wait_recv()

    def send(which, step, index, part, device, to_step):
        push(block(which, step, index, part), block(which, to_step, index, part),
             row_sem.at[which, to_step, index, part], device)

    def take(which, step, index, part):
        await_copy(block(which, step, index, part), row_sem.at[which, step, index, part])

    def to_peers(which, step, index, part):
        for d in range(1, chips):
            send(which, step, index, part, (g, same_core(d)), step)

    def to_next(which, index, part):
        send(which, 0, index, part, (towards[which], m), 1)

    def to_sibling(which, step, index, part):
        send(which, step, index, part, (g, sibling), step)

    for which in range(2):
        to_peers(which, 0, m, 0)
        to_next(which, m, 1)
        to_peers(which, 0, m, 1)
        to_next(which, m, 0)
        for part in range(2):
            to_sibling(which, 0, m, part)

    scale = jnp.exp(jnp.full((rows, 1), log_scale_ref[0], jnp.float32))
    bias = bias_ref[0]
    pair = 2 * rows
    done = [False, False]

    def score(which, step, d):
        low = block(1 - which, 0, m)
        hat = (image_hat, text_hat)[which]
        chip = lax.rem(c + d, chips)
        others = (texts, images)[which][step, pl.ds(pl.multiple_of(chip * pair, pair), pair), :]
        z = scale * lax.dot_general(low[...], others, NT, preferred_element_type=jnp.float32) + bias
        positive = None
        x = z
        if step == 0 and d == 0:
            row = lax.broadcasted_iota(jnp.int32, (rows, pair), 0)
            column = lax.broadcasted_iota(jnp.int32, (rows, pair), 1)
            positive = row + k * rows == column
            x = jnp.where(positive, -z, z)
        e = jnp.exp(-jnp.abs(x))
        coef = jnp.where(x >= 0, 1.0, e) / (1.0 + e)
        if positive is not None:
            coef = jnp.where(positive, -coef, coef)
        update = jnp.dot(coef.astype(jnp.bfloat16), others, preferred_element_type=jnp.float32)
        terms = fold(jnp.maximum(x, 0.0) + jnp.log1p(e)) if which == 0 else None
        if done[which]:
            hat[...] += update
            if which == 0:
                term_sum[...] += terms
        else:
            hat[...] = update
            if which == 0:
                term_sum[...] = terms
        done[which] = True

    def take_sibling(which, step, d):
        for part in range(2):
            take(which, step, 2 * lax.rem(c + d, chips) + 1 - k, part)

    for which in range(2):
        take_sibling(which, 0, 0)
        score(which, 0, 0)

    for which in range(2):
        for d in range(1, chips):
            take(which, 0, same_core(d), 0)
            to_next(which, same_core(d), 0)
            to_sibling(which, 0, same_core(d), 0)
        take(which, 1, m, 1)
        to_peers(which, 1, m, 1)
        to_sibling(which, 1, m, 1)
    for which in range(2):
        for d in range(1, chips):
            take(which, 0, same_core(d), 1)
            to_sibling(which, 0, same_core(d), 1)
        take(which, 1, m, 0)
        to_sibling(which, 1, m, 0)
    for which in range(2):
        for d in range(1, chips):
            take_sibling(which, 0, d)
            score(which, 0, d)
        take_sibling(which, 1, 0)
        score(which, 1, 0)
    for which in range(2):
        for d in range(1, chips):
            for part in (1, 0):
                take(which, 1, same_core(d), part)
                to_sibling(which, 1, same_core(d), part)
    for d in range(1, chips):
        take_sibling(0, 1, d)
        score(0, 1, d)

    group_terms[m] = term_sum[...]
    for d in range(1, n_mp):
        push(group_terms.at[m], group_terms.at[m], group_sem.at[m], (g, peer(d)))
    image_grad_ref[...] = back_norm(scale * image_hat[...], image_ref[...])
    for d in range(1, chips):
        take_sibling(1, 1, d)
        score(1, 1, d)
    for d in range(1, n_mp):
        await_copy(group_terms.at[peer(d)], group_sem.at[peer(d)])
    all_terms[g] = jnp.sum(group_terms[...], axis=0)
    for d in range(1, n_dp):
        push(all_terms.at[g], all_terms.at[g], all_sem.at[g], (ring(d), m))
    text_grad_ref[...] = back_norm(scale * text_hat[...], text_ref[...])
    for d in range(1, n_dp):
        await_copy(all_terms.at[ring(d)], all_sem.at[ring(d)])
    pair_count = n_dp * n_mp * rows * STEPS * n_mp * rows
    loss_ref[0] = jnp.sum(jnp.sum(all_terms[...], axis=0)) / pair_count
    for copy in sends:
        copy.wait_send()


def solution(mesh):
    n_dp, n_mp = mesh.shape["dp"], mesh.shape["mp"]

    def body(image_embed, text_embed, log_scale, logit_bias):
        rows, width = image_embed.shape
        chips = n_mp // 2
        others = chips - 1
        n_sends = 2 * (2 * others + 4) + 2 * (3 * others + 1) + 2 * (others + 1)
        n_sends += 2 * 2 * others + (n_mp - 1) + (n_dp - 1)
        vmem = pl.BlockSpec(memory_space=pltpu.VMEM)
        hbm = pl.BlockSpec(memory_space=pl.ANY)
        smem = pl.BlockSpec(memory_space=pltpu.SMEM)
        grad = jax.ShapeDtypeStruct((rows, width), jnp.float32)
        return pl.pallas_call(
            functools.partial(kernel, n_dp, n_mp),
            out_shape=(jax.ShapeDtypeStruct((1,), jnp.float32), grad, grad),
            in_specs=[hbm, hbm, smem, smem],
            out_specs=(smem, vmem, vmem),
            scratch_shapes=[
                pltpu.VMEM((rows, width), jnp.bfloat16),
                pltpu.VMEM((rows, width), jnp.bfloat16),
                pltpu.VMEM((2, n_mp * rows, width), jnp.bfloat16),
                pltpu.VMEM((2, n_mp * rows, width), jnp.bfloat16),
                pltpu.VMEM((rows, width), jnp.float32),
                pltpu.VMEM((rows, width), jnp.float32),
                pltpu.VMEM((8, 128), jnp.float32),
                pltpu.VMEM((n_mp, 8, 128), jnp.float32),
                pltpu.VMEM((n_dp, 8, 128), jnp.float32),
                pltpu.SemaphoreType.DMA((2,)),
                pltpu.SemaphoreType.DMA((n_sends,)),
                pltpu.SemaphoreType.DMA((2, 2, n_mp, 2)),
                pltpu.SemaphoreType.DMA((n_mp,)),
                pltpu.SemaphoreType.DMA((n_dp,)),
            ],
            compiler_params=pltpu.CompilerParams(
                collective_id=0, has_side_effects=True, vmem_limit_bytes=40 * 1024 * 1024
            ),
        )(image_embed, text_embed, log_scale, logit_bias)

    rows_spec = P(("dp", "mp"), None)
    return jax.shard_map(
        body,
        mesh=mesh,
        in_specs=(rows_spec, rows_spec, P(), P()),
        out_specs=(P(), rows_spec, rows_spec),
        check_vma=False,
    )
```

```python
import functools

import jax
import jax.numpy as jnp
from jax import lax
from jax.experimental import pallas as pl
from jax.experimental.pallas import tpu as pltpu
from jax.sharding import PartitionSpec as P

STEPS = 2
MESH = pl.DeviceIdType.MESH
NT = (((1,), (1,)), ((), ()))


def unit_rows(raw):
    values = raw.astype(jnp.float32)
    norm = jnp.sqrt(jnp.sum(values * values, axis=1, keepdims=True) + 1e-06)
    return (values / norm, norm)


def back_norm(hat, raw):
    unit, norm = unit_rows(raw)
    return (hat - unit * jnp.sum(unit * hat, axis=1, keepdims=True)) / norm


def fold(values):
    rows, columns = values.shape
    tall = values[0:8]
    for r in range(8, rows, 8):
        tall = tall + values[r : r + 8]
    tile = tall[:, 0:128]
    for c in range(128, columns, 128):
        tile = tile + tall[:, c : c + 128]
    return tile


def kernel(
    n_dp, n_mp, image_hbm, text_hbm, log_scale_ref, bias_ref,
    loss_ref, image_grad_ref, text_grad_ref,
    image_ref, text_ref, texts, images, image_hat, text_hat, term_sum, group_terms, all_terms,
    load_sem, send_sem, row_sem, group_sem, all_sem,
):
    rows = image_ref.shape[0]
    chips, half = n_mp // 2, rows // 2
    g, m = lax.axis_index("dp"), lax.axis_index("mp")
    c, k = m // 2, lax.rem(m, 2)
    sibling = 2 * c + 1 - k
    towards = (lax.rem(g + 1, n_dp), lax.rem(g + n_dp - 1, n_dp))

    def same_core(d):
        return 2 * lax.rem(c + d, chips) + k

    def peer(d):
        return lax.rem(m + d, n_mp)

    def ring(d):
        return lax.rem(g + d, n_dp)

    loads = [
        pltpu.make_async_copy(text_hbm, text_ref, load_sem.at[0]),
        pltpu.make_async_copy(image_hbm, image_ref, load_sem.at[1]),
    ]
    for load in loads:
        load.start()

    partners = [(g, peer(d)) for d in range(1, n_mp)]
    partners += [(ring(d), m) for d in range(1, n_dp)]
    barrier = pltpu.get_barrier_semaphore()
    for partner in partners:
        pl.semaphore_signal(barrier, inc=1, device_id=partner, device_id_type=MESH)

    def block(which, step, index, part=None):
        ref = (texts, images)[which]
        if part is None:
            return ref.at[step, pl.ds(pl.multiple_of(index * rows, rows), rows), :]
        start = pl.multiple_of(index * rows + part * half, half)
        return ref.at[step, pl.ds(start, half), :]

    for which, ref in enumerate((text_ref, image_ref)):
        loads[which].wait()
        block(which, 0, m)[...] = unit_rows(ref[...])[0].astype(jnp.bfloat16)
    pl.semaphore_wait(barrier, len(partners))

    sends = []

    def push(src, dst, recv, device):
        copy = pltpu.make_async_remote_copy(
            src_ref=src, dst_ref=dst, send_sem=send_sem.at[len(sends)], recv_sem=recv,
            device_id=device, device_id_type=MESH,
        )
        copy.start()
        sends.append(copy)

    def await_copy(dst, recv):
        pltpu.make_async_remote_copy(
            src_ref=dst, dst_ref=dst, send_sem=send_sem.at[0], recv_sem=recv,
            device_id=(g, sibling), device_id_type=MESH,
        ).wait_recv()

    def send(which, step, index, part, device, to_step):
        push(block(which, step, index, part), block(which, to_step, index, part),
             row_sem.at[which, to_step, index, part], device)

    def take(which, step, index, part):
        await_copy(block(which, step, index, part), row_sem.at[which, step, index, part])

    def to_peers(which, step, index, part):
        for d in range(1, chips):
            send(which, step, index, part, (g, same_core(d)), step)

    def to_next(which, index, part):
        send(which, 0, index, part, (towards[which], m), 1)

    def to_sibling(which, step, index, part):
        send(which, step, index, part, (g, sibling), step)

    def start(*steps):
        first = len(sends)
        for step, *rest in steps:
            step(*rest)
        return first, len(sends)

    def sent(batch):
        for copy in sends[batch[0] : batch[1]]:
            copy.wait_send()
        waited.extend(range(*batch))

    waited = []
    text_0 = start((to_peers, 0, 0, m, 0), (to_next, 0, m, 1))
    text_1 = start((to_peers, 0, 0, m, 1), (to_next, 0, m, 0))
    for which in range(2):
        for part in range(2):
            to_sibling(which, 0, m, part)

    scale = jnp.exp(jnp.full((rows, 1), log_scale_ref[0], jnp.float32))
    bias = bias_ref[0]
    pair = 2 * rows
    done = [False, False]

    def score(which, step, d):
        low = block(1 - which, 0, m)
        hat = (image_hat, text_hat)[which]
        chip = lax.rem(c + d, chips)
        others = (texts, images)[which][step, pl.ds(pl.multiple_of(chip * pair, pair), pair), :]
        z = scale * lax.dot_general(low[...], others, NT, preferred_element_type=jnp.float32) + bias
        positive = None
        x = z
        if step == 0 and d == 0:
            row = lax.broadcasted_iota(jnp.int32, (rows, pair), 0)
            column = lax.broadcasted_iota(jnp.int32, (rows, pair), 1)
            positive = row + k * rows == column
            x = jnp.where(positive, -z, z)
        e = jnp.exp(-jnp.abs(x))
        coef = jnp.where(x >= 0, 1.0, e) / (1.0 + e)
        if positive is not None:
            coef = jnp.where(positive, -coef, coef)
        update = jnp.dot(coef.astype(jnp.bfloat16), others, preferred_element_type=jnp.float32)
        terms = fold(jnp.maximum(x, 0.0) + jnp.log1p(e)) if which == 0 else None
        if done[which]:
            hat[...] += update
            if which == 0:
                term_sum[...] += terms
        else:
            hat[...] = update
            if which == 0:
                term_sum[...] = terms
        done[which] = True

    def take_sibling(which, step, d):
        for part in range(2):
            take(which, step, 2 * lax.rem(c + d, chips) + 1 - k, part)

    for which in range(2):
        take_sibling(which, 0, 0)
        score(which, 0, 0)

    def arrive(which, part):
        for d in range(1, chips):
            take(which, 0, same_core(d), part)
            to_sibling(which, 0, same_core(d), part)
        take(which, 1, m, 1 - part)
        to_sibling(which, 1, m, 1 - part)

    def relay(which):
        steps = [(to_peers, which, 1, m, 1)]
        steps += [(to_next, which, same_core(d), 0) for d in range(1, chips)]
        return start(*steps)

    def last(which):
        for d in range(1, chips):
            for part in range(2):
                take(which, 1, same_core(d), part)
                to_sibling(which, 1, same_core(d), part)

    def score_first(which):
        for d in range(1, chips):
            take_sibling(which, 0, d)
            score(which, 0, d)
        take_sibling(which, 1, 0)
        score(which, 1, 0)

    sent(text_0)
    image_0 = start((to_peers, 1, 0, m, 0), (to_next, 1, m, 1))
    arrive(0, 0)
    sent(text_1)
    text_2 = relay(0)
    arrive(0, 1)
    score_first(0)
    sent(image_0)
    start((to_peers, 1, 0, m, 1), (to_next, 1, m, 0))
    arrive(1, 0)
    sent(text_2)
    relay(1)
    last(0)
    for d in range(1, chips):
        take_sibling(0, 1, d)
        score(0, 1, d)

    group_terms[m] = term_sum[...]
    for d in range(1, n_mp):
        push(group_terms.at[m], group_terms.at[m], group_sem.at[m], (g, peer(d)))
    image_grad_ref[...] = back_norm(scale * image_hat[...], image_ref[...])
    arrive(1, 1)
    for d in range(1, n_mp):
        await_copy(group_terms.at[peer(d)], group_sem.at[peer(d)])
    all_terms[g] = jnp.sum(group_terms[...], axis=0)
    for d in range(1, n_dp):
        push(all_terms.at[g], all_terms.at[g], all_sem.at[g], (ring(d), m))
    score_first(1)
    last(1)
    for d in range(1, chips):
        take_sibling(1, 1, d)
        score(1, 1, d)
    text_grad_ref[...] = back_norm(scale * text_hat[...], text_ref[...])
    for d in range(1, n_dp):
        await_copy(all_terms.at[ring(d)], all_sem.at[ring(d)])
    pair_count = n_dp * n_mp * rows * STEPS * n_mp * rows
    loss_ref[0] = jnp.sum(jnp.sum(all_terms[...], axis=0)) / pair_count
    for index, copy in enumerate(sends):
        if index not in waited:
            copy.wait_send()


def solution(mesh):
    n_dp, n_mp = mesh.shape["dp"], mesh.shape["mp"]

    def body(image_embed, text_embed, log_scale, logit_bias):
        rows, width = image_embed.shape
        chips = n_mp // 2
        others = chips - 1
        n_sends = 2 * (2 * others + 4) + 2 * (3 * others + 1) + 2 * (others + 1)
        n_sends += 2 * 2 * others + (n_mp - 1) + (n_dp - 1)
        vmem = pl.BlockSpec(memory_space=pltpu.VMEM)
        hbm = pl.BlockSpec(memory_space=pl.ANY)
        smem = pl.BlockSpec(memory_space=pltpu.SMEM)
        grad = jax.ShapeDtypeStruct((rows, width), jnp.float32)
        return pl.pallas_call(
            functools.partial(kernel, n_dp, n_mp),
            out_shape=(jax.ShapeDtypeStruct((1,), jnp.float32), grad, grad),
            in_specs=[hbm, hbm, smem, smem],
            out_specs=(smem, vmem, vmem),
            scratch_shapes=[
                pltpu.VMEM((rows, width), jnp.bfloat16),
                pltpu.VMEM((rows, width), jnp.bfloat16),
                pltpu.VMEM((2, n_mp * rows, width), jnp.bfloat16),
                pltpu.VMEM((2, n_mp * rows, width), jnp.bfloat16),
                pltpu.VMEM((rows, width), jnp.float32),
                pltpu.VMEM((rows, width), jnp.float32),
                pltpu.VMEM((8, 128), jnp.float32),
                pltpu.VMEM((n_mp, 8, 128), jnp.float32),
                pltpu.VMEM((n_dp, 8, 128), jnp.float32),
                pltpu.SemaphoreType.DMA((2,)),
                pltpu.SemaphoreType.DMA((n_sends,)),
                pltpu.SemaphoreType.DMA((2, 2, n_mp, 2)),
                pltpu.SemaphoreType.DMA((n_mp,)),
                pltpu.SemaphoreType.DMA((n_dp,)),
            ],
            compiler_params=pltpu.CompilerParams(
                collective_id=0, has_side_effects=True, vmem_limit_bytes=60 * 1024 * 1024
            ),
        )(image_embed, text_embed, log_scale, logit_bias)

    rows_spec = P(("dp", "mp"), None)
    return jax.shard_map(
        body,
        mesh=mesh,
        in_specs=(rows_spec, rows_spec, P(), P()),
        out_specs=(P(), rows_spec, rows_spec),
        check_vma=False,
    )
```

```python
import functools

import jax
import jax.numpy as jnp
from jax import lax
from jax.experimental import pallas as pl
from jax.experimental.pallas import tpu as pltpu
from jax.sharding import PartitionSpec as P

STEPS = 2
MESH = pl.DeviceIdType.MESH
NT = (((1,), (1,)), ((), ()))


def unit_rows(raw):
    values = raw.astype(jnp.float32)
    norm = jnp.sqrt(jnp.sum(values * values, axis=1, keepdims=True) + 1e-06)
    return (values / norm, norm)


def back_norm(hat, raw):
    unit, norm = unit_rows(raw)
    return (hat - unit * jnp.sum(unit * hat, axis=1, keepdims=True)) / norm


def fold(values):
    rows, columns = values.shape
    tall = values[0:8]
    for r in range(8, rows, 8):
        tall = tall + values[r : r + 8]
    tile = tall[:, 0:128]
    for c in range(128, columns, 128):
        tile = tile + tall[:, c : c + 128]
    return tile


def kernel(
    n_dp, n_mp, image_hbm, text_hbm, log_scale_ref, bias_ref,
    loss_ref, image_hat, text_hat,
    image_ref, text_ref, texts, images, term_sum, group_terms, all_terms,
    load_sem, send_sem, row_sem, group_sem, all_sem,
):
    rows = image_ref.shape[0]
    chips, half = n_mp // 2, rows // 2
    g, m = lax.axis_index("dp"), lax.axis_index("mp")
    c, k = m // 2, lax.rem(m, 2)
    sibling = 2 * c + 1 - k
    towards = (lax.rem(g + 1, n_dp), lax.rem(g + n_dp - 1, n_dp))

    def same_core(d):
        return 2 * lax.rem(c + d, chips) + k

    def peer(d):
        return lax.rem(m + d, n_mp)

    def ring(d):
        return lax.rem(g + d, n_dp)

    loads = [
        pltpu.make_async_copy(text_hbm, text_ref, load_sem.at[0]),
        pltpu.make_async_copy(image_hbm, image_ref, load_sem.at[1]),
    ]
    for load in loads:
        load.start()

    partners = [(g, peer(d)) for d in range(1, n_mp)]
    partners += [(ring(d), m) for d in range(1, n_dp)]
    barrier = pltpu.get_barrier_semaphore()
    for partner in partners:
        pl.semaphore_signal(barrier, inc=1, device_id=partner, device_id_type=MESH)

    def block(which, step, index, part=None):
        ref = (texts, images)[which]
        if part is None:
            return ref.at[step, pl.ds(pl.multiple_of(index * rows, rows), rows), :]
        start = pl.multiple_of(index * rows + part * half, half)
        return ref.at[step, pl.ds(start, half), :]

    for which, ref in enumerate((text_ref, image_ref)):
        loads[which].wait()
        block(which, 0, m)[...] = unit_rows(ref[...])[0].astype(jnp.bfloat16)
    pl.semaphore_wait(barrier, len(partners))

    sends = []

    def push(src, dst, recv, device):
        copy = pltpu.make_async_remote_copy(
            src_ref=src, dst_ref=dst, send_sem=send_sem.at[len(sends)], recv_sem=recv,
            device_id=device, device_id_type=MESH,
        )
        copy.start()
        sends.append(copy)

    def await_copy(dst, recv):
        pltpu.make_async_remote_copy(
            src_ref=dst, dst_ref=dst, send_sem=send_sem.at[0], recv_sem=recv,
            device_id=(g, sibling), device_id_type=MESH,
        ).wait_recv()

    def send(which, step, index, part, device, to_step):
        push(block(which, step, index, part), block(which, to_step, index, part),
             row_sem.at[which, to_step, index, part], device)

    def take(which, step, index, part):
        await_copy(block(which, step, index, part), row_sem.at[which, step, index, part])

    def to_peers(which, step, index, part):
        for d in range(1, chips):
            send(which, step, index, part, (g, same_core(d)), step)

    def to_next(which, index, part):
        send(which, 0, index, part, (towards[which], m), 1)

    def to_sibling(which, step, index, part):
        send(which, step, index, part, (g, sibling), step)

    for part in range(2):
        to_peers(0, 0, m, part)
        to_next(0, m, 1 - part)
    for which in range(2):
        for part in range(2):
            to_sibling(which, 0, m, part)

    scale = jnp.exp(jnp.full((rows, 1), log_scale_ref[0], jnp.float32))
    bias = bias_ref[0]
    pair = 2 * rows
    done = [False, False]

    def score(which, step, d):
        low = block(1 - which, 0, m)
        hat = (image_hat, text_hat)[which]
        chip = lax.rem(c + d, chips)
        others = (texts, images)[which][step, pl.ds(pl.multiple_of(chip * pair, pair), pair), :]
        z = scale * lax.dot_general(low[...], others, NT, preferred_element_type=jnp.float32) + bias
        positive = None
        x = z
        if step == 0 and d == 0:
            row = lax.broadcasted_iota(jnp.int32, (rows, pair), 0)
            column = lax.broadcasted_iota(jnp.int32, (rows, pair), 1)
            positive = row + k * rows == column
            x = jnp.where(positive, -z, z)
        e = jnp.exp(-jnp.abs(x))
        coef = jnp.where(x >= 0, 1.0, e) / (1.0 + e)
        if positive is not None:
            coef = jnp.where(positive, -coef, coef)
        update = scale * jnp.dot(
            coef.astype(jnp.bfloat16), others, preferred_element_type=jnp.float32
        )
        terms = fold(jnp.maximum(x, 0.0) + jnp.log1p(e)) if which == 0 else None
        if done[which]:
            hat[...] += update
            if which == 0:
                term_sum[...] += terms
        else:
            hat[...] = update
            if which == 0:
                term_sum[...] = terms
        done[which] = True

    def take_sibling(which, step, d):
        for part in range(2):
            take(which, step, 2 * lax.rem(c + d, chips) + 1 - k, part)

    for which in range(2):
        take_sibling(which, 0, 0)
        score(which, 0, 0)

    def arrive(which, part):
        for d in range(1, chips):
            take(which, 0, same_core(d), part)
            to_sibling(which, 0, same_core(d), part)
        take(which, 1, m, 1 - part)
        to_sibling(which, 1, m, 1 - part)

    def relay(which):
        to_peers(which, 1, m, 1)
        for d in range(1, chips):
            to_next(which, same_core(d), 0)

    def last(which):
        for d in range(1, chips):
            for part in range(2):
                take(which, 1, same_core(d), part)
                to_sibling(which, 1, same_core(d), part)

    def score_first(which):
        for d in range(1, chips):
            take_sibling(which, 0, d)
            score(which, 0, d)
        take_sibling(which, 1, 0)
        score(which, 1, 0)

    for copy in sends[:chips]:
        copy.wait_send()
    for part in range(2):
        to_peers(1, 0, m, part)
        to_next(1, m, 1 - part)
    arrive(0, 0)
    relay(0)
    arrive(0, 1)
    score_first(0)
    arrive(1, 0)
    relay(1)
    last(0)
    for d in range(1, chips):
        take_sibling(0, 1, d)
        score(0, 1, d)

    group_terms[m] = term_sum[...]
    for d in range(1, n_mp):
        push(group_terms.at[m], group_terms.at[m], group_sem.at[m], (g, peer(d)))
    arrive(1, 1)
    for d in range(1, n_mp):
        await_copy(group_terms.at[peer(d)], group_sem.at[peer(d)])
    all_terms[g] = jnp.sum(group_terms[...], axis=0)
    for d in range(1, n_dp):
        push(all_terms.at[g], all_terms.at[g], all_sem.at[g], (ring(d), m))
    score_first(1)
    last(1)
    for d in range(1, chips):
        take_sibling(1, 1, d)
        score(1, 1, d)
    for d in range(1, n_dp):
        await_copy(all_terms.at[ring(d)], all_sem.at[ring(d)])
    pair_count = n_dp * n_mp * rows * STEPS * n_mp * rows
    loss_ref[0] = jnp.sum(jnp.sum(all_terms[...], axis=0)) / pair_count
    for copy in sends[chips:]:
        copy.wait_send()


def finish(image_hat_ref, text_hat_ref, image_ref, text_ref, image_grad_ref, text_grad_ref):
    image_grad_ref[...] = back_norm(image_hat_ref[...], image_ref[...])
    text_grad_ref[...] = back_norm(text_hat_ref[...], text_ref[...])


def solution(mesh):
    n_dp, n_mp = mesh.shape["dp"], mesh.shape["mp"]

    def body(image_embed, text_embed, log_scale, logit_bias):
        rows, width = image_embed.shape
        chips = n_mp // 2
        others = chips - 1
        n_sends = 2 * (2 * others + 4) + 2 * (3 * others + 1) + 2 * (others + 1)
        n_sends += 2 * 2 * others + (n_mp - 1) + (n_dp - 1)
        vmem = pl.BlockSpec(memory_space=pltpu.VMEM)
        hbm = pl.BlockSpec(memory_space=pl.ANY)
        smem = pl.BlockSpec(memory_space=pltpu.SMEM)
        grad = jax.ShapeDtypeStruct((rows, width), jnp.float32)
        loss, image_hat, text_hat = pl.pallas_call(
            functools.partial(kernel, n_dp, n_mp),
            out_shape=(jax.ShapeDtypeStruct((1,), jnp.float32), grad, grad),
            in_specs=[hbm, hbm, smem, smem],
            out_specs=(smem, vmem, vmem),
            scratch_shapes=[
                pltpu.VMEM((rows, width), jnp.bfloat16),
                pltpu.VMEM((rows, width), jnp.bfloat16),
                pltpu.VMEM((2, n_mp * rows, width), jnp.bfloat16),
                pltpu.VMEM((2, n_mp * rows, width), jnp.bfloat16),
                pltpu.VMEM((8, 128), jnp.float32),
                pltpu.VMEM((n_mp, 8, 128), jnp.float32),
                pltpu.VMEM((n_dp, 8, 128), jnp.float32),
                pltpu.SemaphoreType.DMA((2,)),
                pltpu.SemaphoreType.DMA((n_sends,)),
                pltpu.SemaphoreType.DMA((2, 2, n_mp, 2)),
                pltpu.SemaphoreType.DMA((n_mp,)),
                pltpu.SemaphoreType.DMA((n_dp,)),
            ],
            compiler_params=pltpu.CompilerParams(
                collective_id=0, has_side_effects=True, vmem_limit_bytes=60 * 1024 * 1024
            ),
        )(image_embed, text_embed, log_scale, logit_bias)
        tile = pl.BlockSpec((rows // 4, width), lambda i: (i, 0))
        image_grad, text_grad = pl.pallas_call(
            finish,
            grid=(4,),
            out_shape=(grad, grad),
            in_specs=[tile] * 4,
            out_specs=(tile, tile),
            compiler_params=pltpu.CompilerParams(vmem_limit_bytes=60 * 1024 * 1024),
        )(image_hat, text_hat, image_embed, text_embed)
        return loss, image_grad, text_grad

    rows_spec = P(("dp", "mp"), None)
    return jax.shard_map(
        body,
        mesh=mesh,
        in_specs=(rows_spec, rows_spec, P(), P()),
        out_specs=(P(), rows_spec, rows_spec),
        check_vma=False,
    )
```

```python
import functools

import jax
import jax.numpy as jnp
from jax import lax
from jax.experimental import pallas as pl
from jax.experimental.pallas import tpu as pltpu
from jax.sharding import PartitionSpec as P

STEPS = 2
MESH = pl.DeviceIdType.MESH
NT = (((1,), (1,)), ((), ()))


def unit_rows(raw):
    values = raw.astype(jnp.float32)
    norm = jnp.sqrt(jnp.sum(values * values, axis=1, keepdims=True) + 1e-06)
    return (values / norm, norm)


def back_norm(hat, raw):
    unit, norm = unit_rows(raw)
    return (hat - unit * jnp.sum(unit * hat, axis=1, keepdims=True)) / norm


def fold(values):
    rows, columns = values.shape
    tall = values[0:8]
    for r in range(8, rows, 8):
        tall = tall + values[r : r + 8]
    tile = tall[:, 0:128]
    for c in range(128, columns, 128):
        tile = tile + tall[:, c : c + 128]
    return tile


def kernel(
    n_dp, n_mp, image_hbm, text_hbm, log_scale_ref, bias_ref,
    loss_ref, image_grad_ref, text_grad_ref,
    image_ref, text_ref, texts, images, image_hat, text_hat, term_sum, group_terms, all_terms,
    load_sem, send_sem, row_sem, group_sem, all_sem,
):
    rows = image_ref.shape[0]
    chips, half = n_mp // 2, rows // 2
    g, m = lax.axis_index("dp"), lax.axis_index("mp")
    c, k = m // 2, lax.rem(m, 2)
    sibling = 2 * c + 1 - k
    towards = (lax.rem(g + 1, n_dp), lax.rem(g + n_dp - 1, n_dp))

    def same_core(d):
        return 2 * lax.rem(c + d, chips) + k

    def peer(d):
        return lax.rem(m + d, n_mp)

    def ring(d):
        return lax.rem(g + d, n_dp)

    loads = [
        pltpu.make_async_copy(text_hbm, text_ref, load_sem.at[0]),
        pltpu.make_async_copy(image_hbm, image_ref, load_sem.at[1]),
    ]
    for load in loads:
        load.start()

    partners = [(g, peer(d)) for d in range(1, n_mp)]
    partners += [(ring(d), m) for d in range(1, n_dp)]
    barrier = pltpu.get_barrier_semaphore()
    for partner in partners:
        pl.semaphore_signal(barrier, inc=1, device_id=partner, device_id_type=MESH)

    def block(which, step, index, part=None):
        ref = (texts, images)[which]
        if part is None:
            return ref.at[step, pl.ds(pl.multiple_of(index * rows, rows), rows), :]
        start = pl.multiple_of(index * rows + part * half, half)
        return ref.at[step, pl.ds(start, half), :]

    for which, ref in enumerate((text_ref, image_ref)):
        loads[which].wait()
        block(which, 0, m)[...] = unit_rows(ref[...])[0].astype(jnp.bfloat16)
    pl.semaphore_wait(barrier, len(partners))

    sends = []

    def push(src, dst, recv, device):
        copy = pltpu.make_async_remote_copy(
            src_ref=src, dst_ref=dst, send_sem=send_sem.at[len(sends)], recv_sem=recv,
            device_id=device, device_id_type=MESH,
        )
        copy.start()
        sends.append(copy)

    def await_copy(dst, recv):
        pltpu.make_async_remote_copy(
            src_ref=dst, dst_ref=dst, send_sem=send_sem.at[0], recv_sem=recv,
            device_id=(g, sibling), device_id_type=MESH,
        ).wait_recv()

    def send(which, step, index, part, device, to_step):
        push(block(which, step, index, part), block(which, to_step, index, part),
             row_sem.at[which, to_step, index, part], device)

    def take(which, step, index, part):
        await_copy(block(which, step, index, part), row_sem.at[which, step, index, part])

    def to_peers(which, step, index, part):
        for d in range(1, chips):
            send(which, step, index, part, (g, same_core(d)), step)

    def to_next(which, index, part):
        send(which, 0, index, part, (towards[which], m), 1)

    def to_sibling(which, step, index, part):
        send(which, step, index, part, (g, sibling), step)

    for which in range(2):
        for part in range(2):
            to_peers(which, 0, m, part)
            to_next(which, m, 1 - part)
        for part in range(2):
            to_sibling(which, 0, m, part)

    scale = jnp.exp(log_scale_ref[...])
    bias = bias_ref[...]
    pair = 2 * rows
    done = [False, False]

    def score(which, step, d):
        low = block(1 - which, 0, m)
        hat = (image_hat, text_hat)[which]
        chip = lax.rem(c + d, chips)
        others = (texts, images)[which][step, pl.ds(pl.multiple_of(chip * pair, pair), pair), :]
        z = scale * lax.dot_general(low[...], others, NT, preferred_element_type=jnp.float32) + bias
        positive = None
        x = z
        if step == 0 and d == 0:
            row = lax.broadcasted_iota(jnp.int32, (rows, pair), 0)
            column = lax.broadcasted_iota(jnp.int32, (rows, pair), 1)
            positive = row + k * rows == column
            x = jnp.where(positive, -z, z)
        e = jnp.exp(-jnp.abs(x))
        coef = jnp.where(x >= 0, 1.0, e) / (1.0 + e)
        if positive is not None:
            coef = jnp.where(positive, -coef, coef)
        update = jnp.dot(coef.astype(jnp.bfloat16), others, preferred_element_type=jnp.float32)
        terms = fold(jnp.maximum(x, 0.0) + jnp.log1p(e)) if which == 0 else None
        if done[which]:
            hat[...] += update
            if which == 0:
                term_sum[...] += terms
        else:
            hat[...] = update
            if which == 0:
                term_sum[...] = terms
        done[which] = True

    def take_sibling(which, step, d):
        for part in range(2):
            take(which, step, 2 * lax.rem(c + d, chips) + 1 - k, part)

    for which in range(2):
        take_sibling(which, 0, 0)
        score(which, 0, 0)

    def arrive(which, part):
        for d in range(1, chips):
            take(which, 0, same_core(d), part)
            to_sibling(which, 0, same_core(d), part)
        take(which, 1, m, 1 - part)
        to_sibling(which, 1, m, 1 - part)

    def relay(which):
        to_peers(which, 1, m, 1)
        for d in range(1, chips):
            to_next(which, same_core(d), 0)

    def last(which):
        for d in range(1, chips):
            for part in range(2):
                take(which, 1, same_core(d), part)
                to_sibling(which, 1, same_core(d), part)

    def score_first(which):
        for d in range(1, chips):
            take_sibling(which, 0, d)
            score(which, 0, d)
        take_sibling(which, 1, 0)
        score(which, 1, 0)

    for which in range(2):
        arrive(which, 0)
        relay(which)
        arrive(which, 1)
    for which in range(2):
        score_first(which)
    last(0)
    last(1)
    for d in range(1, chips):
        take_sibling(0, 1, d)
        score(0, 1, d)

    group_terms[m] = term_sum[...]
    for d in range(1, n_mp):
        push(group_terms.at[m], group_terms.at[m], group_sem.at[m], (g, peer(d)))
    for d in range(1, chips):
        take_sibling(1, 1, d)
        score(1, 1, d)
    for d in range(1, n_mp):
        await_copy(group_terms.at[peer(d)], group_sem.at[peer(d)])
    all_terms[g] = jnp.sum(group_terms[...], axis=0)
    for d in range(1, n_dp):
        push(all_terms.at[g], all_terms.at[g], all_sem.at[g], (ring(d), m))
    image_grad_ref[...] = back_norm(scale * image_hat[...], image_ref[...])
    text_grad_ref[...] = back_norm(scale * text_hat[...], text_ref[...])
    for d in range(1, n_dp):
        await_copy(all_terms.at[ring(d)], all_sem.at[ring(d)])
    pair_count = n_dp * n_mp * rows * STEPS * n_mp * rows
    loss_ref[0] = jnp.sum(jnp.sum(all_terms[...], axis=0)) / pair_count
    for copy in sends:
        copy.wait_send()


def solution(mesh):
    n_dp, n_mp = mesh.shape["dp"], mesh.shape["mp"]

    def body(image_embed, text_embed, log_scale, logit_bias):
        rows, width = image_embed.shape
        chips = n_mp // 2
        others = chips - 1
        n_sends = 2 * (2 * others + 4) + 2 * (3 * others + 1) + 2 * (others + 1)
        n_sends += 2 * 2 * others + (n_mp - 1) + (n_dp - 1)
        vmem = pl.BlockSpec(memory_space=pltpu.VMEM)
        hbm = pl.BlockSpec(memory_space=pl.ANY)
        smem = pl.BlockSpec(memory_space=pltpu.SMEM)
        grad = jax.ShapeDtypeStruct((rows, width), jnp.float32)
        return pl.pallas_call(
            functools.partial(kernel, n_dp, n_mp),
            out_shape=(jax.ShapeDtypeStruct((1,), jnp.float32), grad, grad),
            in_specs=[hbm, hbm, vmem, vmem],
            out_specs=(smem, vmem, vmem),
            scratch_shapes=[
                pltpu.VMEM((rows, width), jnp.bfloat16),
                pltpu.VMEM((rows, width), jnp.bfloat16),
                pltpu.VMEM((2, n_mp * rows, width), jnp.bfloat16),
                pltpu.VMEM((2, n_mp * rows, width), jnp.bfloat16),
                pltpu.VMEM((rows, width), jnp.float32),
                pltpu.VMEM((rows, width), jnp.float32),
                pltpu.VMEM((8, 128), jnp.float32),
                pltpu.VMEM((n_mp, 8, 128), jnp.float32),
                pltpu.VMEM((n_dp, 8, 128), jnp.float32),
                pltpu.SemaphoreType.DMA((2,)),
                pltpu.SemaphoreType.DMA((n_sends,)),
                pltpu.SemaphoreType.DMA((2, 2, n_mp, 2)),
                pltpu.SemaphoreType.DMA((n_mp,)),
                pltpu.SemaphoreType.DMA((n_dp,)),
            ],
            compiler_params=pltpu.CompilerParams(
                collective_id=0, has_side_effects=True, vmem_limit_bytes=60 * 1024 * 1024
            ),
        )(image_embed, text_embed, log_scale.reshape(1, 1), logit_bias.reshape(1, 1))

    rows_spec = P(("dp", "mp"), None)
    return jax.shard_map(
        body,
        mesh=mesh,
        in_specs=(rows_spec, rows_spec, P(), P()),
        out_specs=(P(), rows_spec, rows_spec),
        check_vma=False,
    )
```

```python
import functools

import jax
import jax.numpy as jnp
from jax import lax
from jax.experimental import pallas as pl
from jax.experimental.pallas import tpu as pltpu
from jax.sharding import PartitionSpec as P

STEPS = 2
MESH = pl.DeviceIdType.MESH
NT = (((1,), (1,)), ((), ()))


def unit_rows(raw):
    values = raw.astype(jnp.float32)
    norm = jnp.sqrt(jnp.sum(values * values, axis=1, keepdims=True) + 1e-06)
    return (values / norm, norm)


def back_norm(hat, raw):
    unit, norm = unit_rows(raw)
    return (hat - unit * jnp.sum(unit * hat, axis=1, keepdims=True)) / norm


def fold(values):
    rows, columns = values.shape
    tall = values[0:8]
    for r in range(8, rows, 8):
        tall = tall + values[r : r + 8]
    tile = tall[:, 0:128]
    for c in range(128, columns, 128):
        tile = tile + tall[:, c : c + 128]
    return tile


def kernel(
    n_dp, n_mp, image_hbm, text_hbm, log_scale_ref, bias_ref,
    loss_ref, image_grad_ref, text_grad_ref,
    image_ref, text_ref, texts, images, image_hat, text_hat, term_sum, group_terms, all_terms,
    load_sem, send_sem, row_sem, group_sem, all_sem,
):
    rows = image_ref.shape[0]
    chips, half = n_mp // 2, rows // 2
    g, m = lax.axis_index("dp"), lax.axis_index("mp")
    c, k = m // 2, lax.rem(m, 2)
    sibling = 2 * c + 1 - k
    towards = (lax.rem(g + 1, n_dp), lax.rem(g + n_dp - 1, n_dp))

    def same_core(d):
        return 2 * lax.rem(c + d, chips) + k

    def peer(d):
        return lax.rem(m + d, n_mp)

    def ring(d):
        return lax.rem(g + d, n_dp)

    loads = [
        pltpu.make_async_copy(text_hbm, text_ref, load_sem.at[0]),
        pltpu.make_async_copy(image_hbm, image_ref, load_sem.at[1]),
    ]
    for load in loads:
        load.start()

    partners = [(g, peer(d)) for d in range(1, n_mp)]
    partners += [(ring(d), m) for d in range(1, n_dp)]
    barrier = pltpu.get_barrier_semaphore()
    for partner in partners:
        pl.semaphore_signal(barrier, inc=1, device_id=partner, device_id_type=MESH)

    def block(which, step, index, part=None):
        ref = (texts, images)[which]
        if part is None:
            return ref.at[step, pl.ds(pl.multiple_of(index * rows, rows), rows), :]
        start = pl.multiple_of(index * rows + part * half, half)
        return ref.at[step, pl.ds(start, half), :]

    def normalise(which):
        loads[which].wait()
        low = unit_rows((text_ref, image_ref)[which][...])[0].astype(jnp.bfloat16)
        block(which, 0, m)[...] = low

    normalise(0)
    pl.semaphore_wait(barrier, len(partners))

    sends = []

    def push(src, dst, recv, device):
        copy = pltpu.make_async_remote_copy(
            src_ref=src, dst_ref=dst, send_sem=send_sem.at[len(sends)], recv_sem=recv,
            device_id=device, device_id_type=MESH,
        )
        copy.start()
        sends.append(copy)

    def await_copy(dst, recv):
        pltpu.make_async_remote_copy(
            src_ref=dst, dst_ref=dst, send_sem=send_sem.at[0], recv_sem=recv,
            device_id=(g, sibling), device_id_type=MESH,
        ).wait_recv()

    def send(which, step, index, part, device, to_step):
        push(block(which, step, index, part), block(which, to_step, index, part),
             row_sem.at[which, to_step, index, part], device)

    def take(which, step, index, part):
        await_copy(block(which, step, index, part), row_sem.at[which, step, index, part])

    def to_peers(which, step, index, part):
        for d in range(1, chips):
            send(which, step, index, part, (g, same_core(d)), step)

    def to_next(which, index, part):
        send(which, 0, index, part, (towards[which], m), 1)

    def to_sibling(which, step, index, part):
        send(which, step, index, part, (g, sibling), step)

    def start(step, *rest):
        first = len(sends)
        step(*rest)
        return sends[first:]

    def sent(copies):
        for copy in copies:
            copy.wait_send()
        waited.extend(copies)

    waited = []
    group_copies, next_copies = [], []
    for part in range(2):
        group_copies.append(start(to_peers, 0, 0, m, part))
        next_copies.append(start(to_next, 0, m, 1 - part))
    for part in range(2):
        to_sibling(0, 0, m, part)
    normalise(1)
    for part in range(2):
        to_sibling(1, 0, m, part)

    scale = jnp.exp(jnp.full((rows, 1), log_scale_ref[0], jnp.float32))
    bias = bias_ref[0]
    pair = 2 * rows
    done = [False, False]

    def score(which, step, d):
        low = block(1 - which, 0, m)
        hat = (image_hat, text_hat)[which]
        chip = lax.rem(c + d, chips)
        others = (texts, images)[which][step, pl.ds(pl.multiple_of(chip * pair, pair), pair), :]
        z = scale * lax.dot_general(low[...], others, NT, preferred_element_type=jnp.float32) + bias
        positive = None
        x = z
        if step == 0 and d == 0:
            row = lax.broadcasted_iota(jnp.int32, (rows, pair), 0)
            column = lax.broadcasted_iota(jnp.int32, (rows, pair), 1)
            positive = row + k * rows == column
            x = jnp.where(positive, -z, z)
        e = jnp.exp(-jnp.abs(x))
        coef = jnp.where(x >= 0, 1.0, e) / (1.0 + e)
        if positive is not None:
            coef = jnp.where(positive, -coef, coef)
        update = jnp.dot(coef.astype(jnp.bfloat16), others, preferred_element_type=jnp.float32)
        terms = fold(jnp.maximum(x, 0.0) + jnp.log1p(e)) if which == 0 else None
        if done[which]:
            hat[...] += update
            if which == 0:
                term_sum[...] += terms
        else:
            hat[...] = update
            if which == 0:
                term_sum[...] = terms
        done[which] = True

    def take_sibling(which, step, d):
        for part in range(2):
            take(which, step, 2 * lax.rem(c + d, chips) + 1 - k, part)

    for which in range(2):
        take_sibling(which, 0, 0)
        score(which, 0, 0)

    def arrive(which, part):
        for d in range(1, chips):
            take(which, 0, same_core(d), part)
            if part == 0:
                to_next(which, same_core(d), 0)
            to_sibling(which, 0, same_core(d), part)
        take(which, 1, m, 1 - part)
        if part == 0:
            to_peers(which, 1, m, 1)
        to_sibling(which, 1, m, 1 - part)

    def last(which):
        for d in range(1, chips):
            for part in range(2):
                take(which, 1, same_core(d), part)
                to_sibling(which, 1, same_core(d), part)

    def score_first(which):
        for d in range(1, chips):
            take_sibling(which, 0, d)
            score(which, 0, d)
        take_sibling(which, 1, 0)
        score(which, 1, 0)

    for part in range(2):
        sent(group_copies[part])
        to_peers(1, 0, m, part)
        sent(next_copies[part])
        to_next(1, m, 1 - part)
        arrive(0, part)
    arrive(1, 0)
    score_first(0)
    last(0)
    for d in range(1, chips):
        take_sibling(0, 1, d)
        score(0, 1, d)

    group_terms[m] = term_sum[...]
    for d in range(1, n_mp):
        push(group_terms.at[m], group_terms.at[m], group_sem.at[m], (g, peer(d)))
    image_grad_ref[...] = back_norm(image_hat[...], image_ref[...])
    arrive(1, 1)
    for d in range(1, n_mp):
        await_copy(group_terms.at[peer(d)], group_sem.at[peer(d)])
    all_terms[g] = jnp.sum(group_terms[...], axis=0)
    for d in range(1, n_dp):
        push(all_terms.at[g], all_terms.at[g], all_sem.at[g], (ring(d), m))
    score_first(1)
    last(1)
    for d in range(1, chips):
        take_sibling(1, 1, d)
        score(1, 1, d)
    text_grad_ref[...] = back_norm(text_hat[...], text_ref[...])
    for d in range(1, n_dp):
        await_copy(all_terms.at[ring(d)], all_sem.at[ring(d)])
    pair_count = n_dp * n_mp * rows * STEPS * n_mp * rows
    loss_ref[0] = jnp.sum(jnp.sum(all_terms[...], axis=0)) / pair_count
    for copy in sends:
        if not any(copy is other for other in waited):
            copy.wait_send()


def solution(mesh):
    n_dp, n_mp = mesh.shape["dp"], mesh.shape["mp"]

    def body(image_embed, text_embed, log_scale, logit_bias):
        rows, width = image_embed.shape
        chips = n_mp // 2
        others = chips - 1
        n_sends = 2 * (2 * others + 4) + 2 * (3 * others + 1) + 2 * (others + 1)
        n_sends += 2 * 2 * others + (n_mp - 1) + (n_dp - 1)
        vmem = pl.BlockSpec(memory_space=pltpu.VMEM)
        hbm = pl.BlockSpec(memory_space=pl.ANY)
        smem = pl.BlockSpec(memory_space=pltpu.SMEM)
        grad = jax.ShapeDtypeStruct((rows, width), jnp.float32)
        loss, image_grad, text_grad = pl.pallas_call(
            functools.partial(kernel, n_dp, n_mp),
            out_shape=(jax.ShapeDtypeStruct((1,), jnp.float32), grad, grad),
            in_specs=[hbm, hbm, smem, smem],
            out_specs=(smem, vmem, vmem),
            scratch_shapes=[
                pltpu.VMEM((rows, width), jnp.bfloat16),
                pltpu.VMEM((rows, width), jnp.bfloat16),
                pltpu.VMEM((2, n_mp * rows, width), jnp.bfloat16),
                pltpu.VMEM((2, n_mp * rows, width), jnp.bfloat16),
                pltpu.VMEM((rows, width), jnp.float32),
                pltpu.VMEM((rows, width), jnp.float32),
                pltpu.VMEM((8, 128), jnp.float32),
                pltpu.VMEM((n_mp, 8, 128), jnp.float32),
                pltpu.VMEM((n_dp, 8, 128), jnp.float32),
                pltpu.SemaphoreType.DMA((2,)),
                pltpu.SemaphoreType.DMA((n_sends,)),
                pltpu.SemaphoreType.DMA((2, 2, n_mp, 2)),
                pltpu.SemaphoreType.DMA((n_mp,)),
                pltpu.SemaphoreType.DMA((n_dp,)),
            ],
            compiler_params=pltpu.CompilerParams(
                collective_id=0, has_side_effects=True, vmem_limit_bytes=60 * 1024 * 1024
            ),
        )(image_embed, text_embed, log_scale, logit_bias)
        scale = jnp.exp(log_scale[0])
        return loss, scale * image_grad, scale * text_grad

    rows_spec = P(("dp", "mp"), None)
    return jax.shard_map(
        body,
        mesh=mesh,
        in_specs=(rows_spec, rows_spec, P(), P()),
        out_specs=(P(), rows_spec, rows_spec),
        check_vma=False,
    )
```

```python
import functools

import jax
import jax.numpy as jnp
from jax import lax
from jax.experimental import pallas as pl
from jax.experimental.pallas import tpu as pltpu
from jax.sharding import PartitionSpec as P

STEPS = 2
MESH = pl.DeviceIdType.MESH
NT = (((1,), (1,)), ((), ()))


def unit_rows(raw):
    values = raw.astype(jnp.float32)
    norm = jnp.sqrt(jnp.sum(values * values, axis=1, keepdims=True) + 1e-06)
    return (values / norm, norm)


def back_norm(hat, raw):
    unit, norm = unit_rows(raw)
    return (hat - unit * jnp.sum(unit * hat, axis=1, keepdims=True)) / norm


def fold(values):
    rows, columns = values.shape
    tall = values[0:8]
    for r in range(8, rows, 8):
        tall = tall + values[r : r + 8]
    tile = tall[:, 0:128]
    for c in range(128, columns, 128):
        tile = tile + tall[:, c : c + 128]
    return tile


def kernel(
    n_dp, n_mp, image_hbm, text_hbm, log_scale_ref, bias_ref,
    loss_ref, image_grad_ref, text_grad_ref,
    image_ref, text_ref, texts, images, image_hat, text_hat, term_sum, group_terms, all_terms,
    load_sem, send_sem, row_sem, group_sem, all_sem,
):
    rows = image_ref.shape[0]
    chips, half = n_mp // 2, rows // 2
    g, m = lax.axis_index("dp"), lax.axis_index("mp")
    c, k = m // 2, lax.rem(m, 2)
    sibling = 2 * c + 1 - k
    towards = (lax.rem(g + 1, n_dp), lax.rem(g + n_dp - 1, n_dp))

    def same_core(d):
        return 2 * lax.rem(c + d, chips) + k

    def peer(d):
        return lax.rem(m + d, n_mp)

    def ring(d):
        return lax.rem(g + d, n_dp)

    loads = [
        pltpu.make_async_copy(text_hbm, text_ref, load_sem.at[0]),
        pltpu.make_async_copy(image_hbm, image_ref, load_sem.at[1]),
    ]
    for load in loads:
        load.start()

    partners = [(g, peer(d)) for d in range(1, n_mp)]
    partners += [(ring(d), m) for d in range(1, n_dp)]
    barrier = pltpu.get_barrier_semaphore()
    for partner in partners:
        pl.semaphore_signal(barrier, inc=1, device_id=partner, device_id_type=MESH)

    def block(which, step, index, part=None):
        ref = (texts, images)[which]
        if part is None:
            return ref.at[step, pl.ds(pl.multiple_of(index * rows, rows), rows), :]
        start = pl.multiple_of(index * rows + part * half, half)
        return ref.at[step, pl.ds(start, half), :]

    def normalise(which):
        loads[which].wait()
        low = unit_rows((text_ref, image_ref)[which][...])[0].astype(jnp.bfloat16)
        block(which, 0, m)[...] = low

    normalise(0)
    pl.semaphore_wait(barrier, len(partners))

    sends, held = [], []

    def push(src, dst, recv, device):
        copy = pltpu.make_async_remote_copy(
            src_ref=src, dst_ref=dst, send_sem=send_sem.at[len(sends)], recv_sem=recv,
            device_id=device, device_id_type=MESH,
        )
        sends.append(copy)
        if not held:
            copy.start()

    def await_copy(dst, recv):
        pltpu.make_async_remote_copy(
            src_ref=dst, dst_ref=dst, send_sem=send_sem.at[0], recv_sem=recv,
            device_id=(g, sibling), device_id_type=MESH,
        ).wait_recv()

    def send(which, step, index, part, device, to_step):
        push(block(which, step, index, part), block(which, to_step, index, part),
             row_sem.at[which, to_step, index, part], device)

    def take(which, step, index, part):
        await_copy(block(which, step, index, part), row_sem.at[which, step, index, part])

    def to_peers(which, step, index, part):
        for d in range(1, chips):
            send(which, step, index, part, (g, same_core(d)), step)

    def to_next(which, index, part):
        send(which, 0, index, part, (towards[which], m), 1)

    def to_sibling(which, step, index, part):
        send(which, step, index, part, (g, sibling), step)

    def made(step, *rest):
        held.append(True)
        first = len(sends)
        step(*rest)
        held.pop()
        return sends[first:]

    def start_both(one, two):
        for core, order in enumerate((one + two, two + one)):
            @pl.when(k == core)
            def _():
                for copy in order:
                    copy.start()

    def sent(copies):
        for copy in copies:
            copy.wait_send()
        waited.extend(copies)

    waited = []
    group_copies, next_copies = [], []
    for part in range(2):
        group_copies.append(made(to_peers, 0, 0, m, part))
        next_copies.append(made(to_next, 0, m, 1 - part))
        start_both(group_copies[part], next_copies[part])
    for part in range(2):
        to_sibling(0, 0, m, part)
    normalise(1)
    for part in range(2):
        to_sibling(1, 0, m, part)

    scale = jnp.exp(jnp.full((rows, 1), log_scale_ref[0], jnp.float32))
    bias = bias_ref[0]
    pair = 2 * rows
    done = [False, False]

    def score(which, step, d, core=None):
        low = block(1 - which, 0, m)
        hat = (image_hat, text_hat)[which]
        chip = lax.rem(c + d, chips)
        if core is None:
            others = (texts, images)[which][step, pl.ds(pl.multiple_of(chip * pair, pair), pair), :]
        else:
            others = block(which, step, 2 * chip + core)[...]
        z = scale * lax.dot_general(low[...], others, NT, preferred_element_type=jnp.float32) + bias
        positive = None
        x = z
        if step == 0 and d == 0:
            row = lax.broadcasted_iota(jnp.int32, (rows, pair), 0)
            column = lax.broadcasted_iota(jnp.int32, (rows, pair), 1)
            positive = row + k * rows == column
            x = jnp.where(positive, -z, z)
        e = jnp.exp(-jnp.abs(x))
        coef = jnp.where(x >= 0, 1.0, e) / (1.0 + e)
        if positive is not None:
            coef = jnp.where(positive, -coef, coef)
        update = jnp.dot(coef.astype(jnp.bfloat16), others, preferred_element_type=jnp.float32)
        terms = fold(jnp.maximum(x, 0.0) + jnp.log1p(e)) if which == 0 else None
        if done[which]:
            hat[...] += update
            if which == 0:
                term_sum[...] += terms
        else:
            hat[...] = update
            if which == 0:
                term_sum[...] = terms
        done[which] = True

    def take_sibling(which, step, d):
        for part in range(2):
            take(which, step, 2 * lax.rem(c + d, chips) + 1 - k, part)

    for which in range(2):
        take_sibling(which, 0, 0)
        score(which, 0, 0)

    def arrive(which, part):
        for d in range(1, chips):
            take(which, 0, same_core(d), part)
            if part == 0:
                to_next(which, same_core(d), 0)
            to_sibling(which, 0, same_core(d), part)
        take(which, 1, m, 1 - part)
        if part == 0:
            to_peers(which, 1, m, 1)
        to_sibling(which, 1, m, 1 - part)

    def last(which):
        for d in range(1, chips):
            for part in range(2):
                take(which, 1, same_core(d), part)
                to_sibling(which, 1, same_core(d), part)

    def score_first(which):
        for d in range(1, chips):
            take_sibling(which, 0, d)
            score(which, 0, d)
        take_sibling(which, 1, 0)
        score(which, 1, 0)

    for part in range(2):
        sent(group_copies[part])
        sent(next_copies[part])
        start_both(made(to_peers, 1, 0, m, part), made(to_next, 1, m, 1 - part))
        arrive(0, part)
    arrive(1, 0)
    score_first(0)
    last(0)
    for d in range(1, chips):
        score(0, 1, d, k)
        take_sibling(0, 1, d)
        score(0, 1, d, 1 - k)

    group_terms[m] = term_sum[...]
    for d in range(1, n_mp):
        push(group_terms.at[m], group_terms.at[m], group_sem.at[m], (g, peer(d)))
    image_grad_ref[...] = back_norm(image_hat[...], image_ref[...])
    arrive(1, 1)
    for d in range(1, n_mp):
        await_copy(group_terms.at[peer(d)], group_sem.at[peer(d)])
    all_terms[g] = jnp.sum(group_terms[...], axis=0)
    for d in range(1, n_dp):
        push(all_terms.at[g], all_terms.at[g], all_sem.at[g], (ring(d), m))
    score_first(1)
    last(1)
    for d in range(1, chips):
        score(1, 1, d, k)
        take_sibling(1, 1, d)
        score(1, 1, d, 1 - k)
    text_grad_ref[...] = back_norm(text_hat[...], text_ref[...])
    for d in range(1, n_dp):
        await_copy(all_terms.at[ring(d)], all_sem.at[ring(d)])
    pair_count = n_dp * n_mp * rows * STEPS * n_mp * rows
    loss_ref[0] = jnp.sum(jnp.sum(all_terms[...], axis=0)) / pair_count
    for copy in sends:
        if not any(copy is other for other in waited):
            copy.wait_send()


def solution(mesh):
    n_dp, n_mp = mesh.shape["dp"], mesh.shape["mp"]

    def body(image_embed, text_embed, log_scale, logit_bias):
        rows, width = image_embed.shape
        chips = n_mp // 2
        others = chips - 1
        n_sends = 2 * (2 * others + 4) + 2 * (3 * others + 1) + 2 * (others + 1)
        n_sends += 2 * 2 * others + (n_mp - 1) + (n_dp - 1)
        vmem = pl.BlockSpec(memory_space=pltpu.VMEM)
        hbm = pl.BlockSpec(memory_space=pl.ANY)
        smem = pl.BlockSpec(memory_space=pltpu.SMEM)
        grad = jax.ShapeDtypeStruct((rows, width), jnp.float32)
        loss, image_grad, text_grad = pl.pallas_call(
            functools.partial(kernel, n_dp, n_mp),
            out_shape=(jax.ShapeDtypeStruct((1,), jnp.float32), grad, grad),
            in_specs=[hbm, hbm, smem, smem],
            out_specs=(smem, vmem, vmem),
            scratch_shapes=[
                pltpu.VMEM((rows, width), jnp.bfloat16),
                pltpu.VMEM((rows, width), jnp.bfloat16),
                pltpu.VMEM((2, n_mp * rows, width), jnp.bfloat16),
                pltpu.VMEM((2, n_mp * rows, width), jnp.bfloat16),
                pltpu.VMEM((rows, width), jnp.float32),
                pltpu.VMEM((rows, width), jnp.float32),
                pltpu.VMEM((8, 128), jnp.float32),
                pltpu.VMEM((n_mp, 8, 128), jnp.float32),
                pltpu.VMEM((n_dp, 8, 128), jnp.float32),
                pltpu.SemaphoreType.DMA((2,)),
                pltpu.SemaphoreType.DMA((n_sends,)),
                pltpu.SemaphoreType.DMA((2, 2, n_mp, 2)),
                pltpu.SemaphoreType.DMA((n_mp,)),
                pltpu.SemaphoreType.DMA((n_dp,)),
            ],
            compiler_params=pltpu.CompilerParams(
                collective_id=0, has_side_effects=True, vmem_limit_bytes=60 * 1024 * 1024
            ),
        )(image_embed, text_embed, log_scale, logit_bias)
        scale = jnp.exp(log_scale[0])
        return loss, scale * image_grad, scale * text_grad

    rows_spec = P(("dp", "mp"), None)
    return jax.shard_map(
        body,
        mesh=mesh,
        in_specs=(rows_spec, rows_spec, P(), P()),
        out_specs=(P(), rows_spec, rows_spec),
        check_vma=False,
    )
```

```python
import functools

import jax
import jax.numpy as jnp
from jax import lax
from jax.experimental import pallas as pl
from jax.experimental.pallas import tpu as pltpu
from jax.sharding import PartitionSpec as P

STEPS = 2
MESH = pl.DeviceIdType.MESH
NT = (((1,), (1,)), ((), ()))


def unit_rows(raw):
    values = raw.astype(jnp.float32)
    norm = jnp.sqrt(jnp.sum(values * values, axis=1, keepdims=True) + 1e-06)
    return (values / norm, norm)


def back_norm(hat, raw):
    unit, norm = unit_rows(raw)
    return (hat - unit * jnp.sum(unit * hat, axis=1, keepdims=True)) / norm


def fold(values):
    rows, columns = values.shape
    tall = values[0:8]
    for r in range(8, rows, 8):
        tall = tall + values[r : r + 8]
    tile = tall[:, 0:128]
    for c in range(128, columns, 128):
        tile = tile + tall[:, c : c + 128]
    return tile


def kernel(
    n_dp, n_mp, image_hbm, text_hbm, log_scale_ref, bias_ref,
    loss_ref, image_grad_ref, text_grad_ref,
    image_ref, text_ref, texts, images, image_hat, text_hat, term_sum, group_terms, all_terms,
    load_sem, send_sem, row_sem, group_sem, all_sem,
):
    rows = image_ref.shape[0]
    chips, cut = n_mp // 2, rows * 3 // 8
    g, m = lax.axis_index("dp"), lax.axis_index("mp")
    c, k = m // 2, lax.rem(m, 2)
    sibling = 2 * c + 1 - k
    towards = (lax.rem(g + 1, n_dp), lax.rem(g + n_dp - 1, n_dp))

    def same_core(d):
        return 2 * lax.rem(c + d, chips) + k

    def peer(d):
        return lax.rem(m + d, n_mp)

    def ring(d):
        return lax.rem(g + d, n_dp)

    loads = [
        pltpu.make_async_copy(text_hbm, text_ref, load_sem.at[0]),
        pltpu.make_async_copy(image_hbm, image_ref, load_sem.at[1]),
    ]
    for load in loads:
        load.start()

    partners = [(g, peer(d)) for d in range(1, n_mp)]
    partners += [(ring(d), m) for d in range(1, n_dp)]
    barrier = pltpu.get_barrier_semaphore()
    for partner in partners:
        pl.semaphore_signal(barrier, inc=1, device_id=partner, device_id_type=MESH)

    def block(which, step, index, part=None):
        ref = (texts, images)[which]
        if part is None:
            return ref.at[step, pl.ds(pl.multiple_of(index * rows, rows), rows), :]
        start = pl.multiple_of(index * rows + part * cut, 16)
        return ref.at[step, pl.ds(start, (cut, rows - cut)[part]), :]

    def normalise(which):
        loads[which].wait()
        low = unit_rows((text_ref, image_ref)[which][...])[0].astype(jnp.bfloat16)
        block(which, 0, m)[...] = low

    normalise(0)
    pl.semaphore_wait(barrier, len(partners))

    sends, held = [], []

    def push(src, dst, recv, device):
        copy = pltpu.make_async_remote_copy(
            src_ref=src, dst_ref=dst, send_sem=send_sem.at[len(sends)], recv_sem=recv,
            device_id=device, device_id_type=MESH,
        )
        sends.append(copy)
        if not held:
            copy.start()

    def await_copy(dst, recv):
        pltpu.make_async_remote_copy(
            src_ref=dst, dst_ref=dst, send_sem=send_sem.at[0], recv_sem=recv,
            device_id=(g, sibling), device_id_type=MESH,
        ).wait_recv()

    def send(which, step, index, part, device, to_step):
        push(block(which, step, index, part), block(which, to_step, index, part),
             row_sem.at[which, to_step, index, part], device)

    def take(which, step, index, part):
        await_copy(block(which, step, index, part), row_sem.at[which, step, index, part])

    def to_peers(which, step, index, part):
        for d in range(1, chips):
            send(which, step, index, part, (g, same_core(d)), step)

    def to_next(which, index, part):
        send(which, 0, index, part, (towards[which], m), 1)

    def to_sibling(which, step, index, part):
        send(which, step, index, part, (g, sibling), step)

    def made(step, *rest):
        held.append(True)
        first = len(sends)
        step(*rest)
        held.pop()
        return sends[first:]

    def start_both(one, two):
        for core, order in enumerate((one + two, two + one)):
            @pl.when(k == core)
            def _():
                for copy in order:
                    copy.start()

    def sent(copies):
        for copy in copies:
            copy.wait_send()
        waited.extend(copies)

    waited = []
    group_copies, next_copies = [], []
    for part in range(2):
        group_copies.append(made(to_peers, 0, 0, m, part))
        next_copies.append(made(to_next, 0, m, 1 - part))
        start_both(group_copies[part], next_copies[part])
    for part in range(2):
        to_sibling(0, 0, m, part)
    normalise(1)
    for part in range(2):
        to_sibling(1, 0, m, part)

    scale = jnp.exp(jnp.full((rows, 1), log_scale_ref[0], jnp.float32))
    bias = bias_ref[0]
    pair = 2 * rows
    done = [False, False]

    def score(which, step, d, core=None):
        low = block(1 - which, 0, m)
        hat = (image_hat, text_hat)[which]
        chip = lax.rem(c + d, chips)
        if core is None:
            others = (texts, images)[which][step, pl.ds(pl.multiple_of(chip * pair, pair), pair), :]
        else:
            others = block(which, step, 2 * chip + core)[...]
        z = scale * lax.dot_general(low[...], others, NT, preferred_element_type=jnp.float32) + bias
        positive = None
        x = z
        if step == 0 and d == 0:
            row = lax.broadcasted_iota(jnp.int32, (rows, pair), 0)
            column = lax.broadcasted_iota(jnp.int32, (rows, pair), 1)
            positive = row + k * rows == column
            x = jnp.where(positive, -z, z)
        e = jnp.exp(-jnp.abs(x))
        coef = jnp.where(x >= 0, 1.0, e) / (1.0 + e)
        if positive is not None:
            coef = jnp.where(positive, -coef, coef)
        update = jnp.dot(coef.astype(jnp.bfloat16), others, preferred_element_type=jnp.float32)
        terms = fold(jnp.maximum(x, 0.0) + jnp.log1p(e)) if which == 0 else None
        if done[which]:
            hat[...] += update
            if which == 0:
                term_sum[...] += terms
        else:
            hat[...] = update
            if which == 0:
                term_sum[...] = terms
        done[which] = True

    def take_sibling(which, step, d):
        for part in range(2):
            take(which, step, 2 * lax.rem(c + d, chips) + 1 - k, part)

    for which in range(2):
        take_sibling(which, 0, 0)
        score(which, 0, 0)

    def arrive(which, part):
        for d in range(1, chips):
            take(which, 0, same_core(d), part)
            if part == 0:
                to_next(which, same_core(d), 0)
            to_sibling(which, 0, same_core(d), part)
        take(which, 1, m, 1 - part)
        if part == 0:
            to_peers(which, 1, m, 1)
        to_sibling(which, 1, m, 1 - part)

    def last(which):
        for d in range(1, chips):
            for part in range(2):
                take(which, 1, same_core(d), part)
                to_sibling(which, 1, same_core(d), part)

    def score_first(which):
        for d in range(1, chips):
            take_sibling(which, 0, d)
            score(which, 0, d)
        take_sibling(which, 1, 0)
        score(which, 1, 0)

    for part in range(2):
        sent(group_copies[part])
        sent(next_copies[part])
        start_both(made(to_peers, 1, 0, m, part), made(to_next, 1, m, 1 - part))
        arrive(0, part)
    arrive(1, 0)
    score_first(0)
    last(0)
    for d in range(1, chips):
        score(0, 1, d, k)
        take_sibling(0, 1, d)
        score(0, 1, d, 1 - k)

    group_terms[m] = term_sum[...]
    for d in range(1, n_mp):
        push(group_terms.at[m], group_terms.at[m], group_sem.at[m], (g, peer(d)))
    image_grad_ref[...] = back_norm(image_hat[...], image_ref[...])
    arrive(1, 1)
    for d in range(1, n_mp):
        await_copy(group_terms.at[peer(d)], group_sem.at[peer(d)])
    all_terms[g] = jnp.sum(group_terms[...], axis=0)
    for d in range(1, n_dp):
        push(all_terms.at[g], all_terms.at[g], all_sem.at[g], (ring(d), m))
    score_first(1)
    last(1)
    for d in range(1, chips):
        score(1, 1, d, k)
        take_sibling(1, 1, d)
        score(1, 1, d, 1 - k)
    text_grad_ref[...] = back_norm(text_hat[...], text_ref[...])
    for d in range(1, n_dp):
        await_copy(all_terms.at[ring(d)], all_sem.at[ring(d)])
    pair_count = n_dp * n_mp * rows * STEPS * n_mp * rows
    loss_ref[0] = jnp.sum(jnp.sum(all_terms[...], axis=0)) / pair_count
    for copy in sends:
        if not any(copy is other for other in waited):
            copy.wait_send()


def solution(mesh):
    n_dp, n_mp = mesh.shape["dp"], mesh.shape["mp"]

    def body(image_embed, text_embed, log_scale, logit_bias):
        rows, width = image_embed.shape
        chips = n_mp // 2
        others = chips - 1
        n_sends = 2 * (2 * others + 4) + 2 * (3 * others + 1) + 2 * (others + 1)
        n_sends += 2 * 2 * others + (n_mp - 1) + (n_dp - 1)
        vmem = pl.BlockSpec(memory_space=pltpu.VMEM)
        hbm = pl.BlockSpec(memory_space=pl.ANY)
        smem = pl.BlockSpec(memory_space=pltpu.SMEM)
        grad = jax.ShapeDtypeStruct((rows, width), jnp.float32)
        loss, image_grad, text_grad = pl.pallas_call(
            functools.partial(kernel, n_dp, n_mp),
            out_shape=(jax.ShapeDtypeStruct((1,), jnp.float32), grad, grad),
            in_specs=[hbm, hbm, smem, smem],
            out_specs=(smem, vmem, vmem),
            scratch_shapes=[
                pltpu.VMEM((rows, width), jnp.bfloat16),
                pltpu.VMEM((rows, width), jnp.bfloat16),
                pltpu.VMEM((2, n_mp * rows, width), jnp.bfloat16),
                pltpu.VMEM((2, n_mp * rows, width), jnp.bfloat16),
                pltpu.VMEM((rows, width), jnp.float32),
                pltpu.VMEM((rows, width), jnp.float32),
                pltpu.VMEM((8, 128), jnp.float32),
                pltpu.VMEM((n_mp, 8, 128), jnp.float32),
                pltpu.VMEM((n_dp, 8, 128), jnp.float32),
                pltpu.SemaphoreType.DMA((2,)),
                pltpu.SemaphoreType.DMA((n_sends,)),
                pltpu.SemaphoreType.DMA((2, 2, n_mp, 2)),
                pltpu.SemaphoreType.DMA((n_mp,)),
                pltpu.SemaphoreType.DMA((n_dp,)),
            ],
            compiler_params=pltpu.CompilerParams(
                collective_id=0, has_side_effects=True, vmem_limit_bytes=60 * 1024 * 1024
            ),
        )(image_embed, text_embed, log_scale, logit_bias)
        scale = jnp.exp(log_scale[0])
        return loss, scale * image_grad, scale * text_grad

    rows_spec = P(("dp", "mp"), None)
    return jax.shard_map(
        body,
        mesh=mesh,
        in_specs=(rows_spec, rows_spec, P(), P()),
        out_specs=(P(), rows_spec, rows_spec),
        check_vma=False,
    )
```

```python
import functools

import jax
import jax.numpy as jnp
from jax import lax
from jax.experimental import pallas as pl
from jax.experimental.pallas import tpu as pltpu
from jax.sharding import PartitionSpec as P

STEPS = 2
MESH = pl.DeviceIdType.MESH
NT = (((1,), (1,)), ((), ()))


def unit_rows(raw):
    values = raw.astype(jnp.float32)
    norm = jnp.sqrt(jnp.sum(values * values, axis=1, keepdims=True) + 1e-06)
    return (values / norm, norm)


def back_norm(hat, raw):
    unit, norm = unit_rows(raw)
    return (hat - unit * jnp.sum(unit * hat, axis=1, keepdims=True)) / norm


def fold(values):
    rows, columns = values.shape
    tall = values[0:8]
    for r in range(8, rows, 8):
        tall = tall + values[r : r + 8]
    tile = tall[:, 0:128]
    for c in range(128, columns, 128):
        tile = tile + tall[:, c : c + 128]
    return tile


def kernel(
    n_dp, n_mp, image_hbm, text_hbm, log_scale_ref, bias_ref,
    loss_ref, image_grad_ref, text_grad_ref,
    image_ref, text_ref, texts, images, image_hat, text_hat, term_sum, group_terms, all_terms,
    load_sem, send_sem, row_sem, group_sem, all_sem,
):
    rows = image_ref.shape[0]
    chips, cut = n_mp // 2, rows // 8
    g, m = lax.axis_index("dp"), lax.axis_index("mp")
    c, k = m // 2, lax.rem(m, 2)
    sibling = 2 * c + 1 - k
    towards = (lax.rem(g + 1, n_dp), lax.rem(g + n_dp - 1, n_dp))

    def same_core(d):
        return 2 * lax.rem(c + d, chips) + k

    def peer(d):
        return lax.rem(m + d, n_mp)

    def ring(d):
        return lax.rem(g + d, n_dp)

    loads = [
        pltpu.make_async_copy(text_hbm, text_ref, load_sem.at[0]),
        pltpu.make_async_copy(image_hbm, image_ref, load_sem.at[1]),
    ]
    for load in loads:
        load.start()

    partners = [(g, peer(d)) for d in range(1, n_mp)]
    partners += [(ring(d), m) for d in range(1, n_dp)]
    barrier = pltpu.get_barrier_semaphore()
    for partner in partners:
        pl.semaphore_signal(barrier, inc=1, device_id=partner, device_id_type=MESH)

    def block(which, step, index, part=None):
        ref = (texts, images)[which]
        if part is None:
            return ref.at[step, pl.ds(pl.multiple_of(index * rows, rows), rows), :]
        start = pl.multiple_of(index * rows + part * cut, 16)
        return ref.at[step, pl.ds(start, (cut, rows - cut)[part]), :]

    def normalise(which):
        loads[which].wait()
        low = unit_rows((text_ref, image_ref)[which][...])[0].astype(jnp.bfloat16)
        block(which, 0, m)[...] = low

    normalise(0)
    pl.semaphore_wait(barrier, len(partners))

    sends, held = [], []

    def push(src, dst, recv, device):
        copy = pltpu.make_async_remote_copy(
            src_ref=src, dst_ref=dst, send_sem=send_sem.at[len(sends)], recv_sem=recv,
            device_id=device, device_id_type=MESH,
        )
        sends.append(copy)
        if not held:
            copy.start()

    def await_copy(dst, recv):
        pltpu.make_async_remote_copy(
            src_ref=dst, dst_ref=dst, send_sem=send_sem.at[0], recv_sem=recv,
            device_id=(g, sibling), device_id_type=MESH,
        ).wait_recv()

    def send(which, step, index, part, device, to_step):
        push(block(which, step, index, part), block(which, to_step, index, part),
             row_sem.at[which, to_step, index, part], device)

    def take(which, step, index, part):
        await_copy(block(which, step, index, part), row_sem.at[which, step, index, part])

    def to_peers(which, step, index, part):
        for d in range(1, chips):
            send(which, step, index, part, (g, same_core(d)), step)

    def to_next(which, index, part):
        send(which, 0, index, part, (towards[which], m), 1)

    def to_sibling(which, step, index, part):
        send(which, step, index, part, (g, sibling), step)

    def made(step, *rest):
        held.append(True)
        first = len(sends)
        step(*rest)
        held.pop()
        return sends[first:]

    def start_both(one, two):
        for core, order in enumerate((one + two, two + one)):
            @pl.when(k == core)
            def _():
                for copy in order:
                    copy.start()

    def sent(copies):
        for copy in copies:
            copy.wait_send()
        waited.extend(copies)

    waited = []
    group_copies, next_copies = [], []
    for part in range(2):
        group_copies.append(made(to_peers, 0, 0, m, part))
        next_copies.append(made(to_next, 0, m, 1 - part))
        start_both(group_copies[part], next_copies[part])
    for part in range(2):
        to_sibling(0, 0, m, part)
    normalise(1)
    for part in range(2):
        to_sibling(1, 0, m, part)

    scale = jnp.exp(jnp.full((rows, 1), log_scale_ref[0], jnp.float32))
    bias = bias_ref[0]
    pair = 2 * rows
    done = [False, False]

    def score(which, step, d, core=None):
        low = block(1 - which, 0, m)
        hat = (image_hat, text_hat)[which]
        chip = lax.rem(c + d, chips)
        if core is None:
            others = (texts, images)[which][step, pl.ds(pl.multiple_of(chip * pair, pair), pair), :]
        else:
            others = block(which, step, 2 * chip + core)[...]
        z = scale * lax.dot_general(low[...], others, NT, preferred_element_type=jnp.float32) + bias
        positive = None
        x = z
        if step == 0 and d == 0:
            row = lax.broadcasted_iota(jnp.int32, (rows, pair), 0)
            column = lax.broadcasted_iota(jnp.int32, (rows, pair), 1)
            positive = row + k * rows == column
            x = jnp.where(positive, -z, z)
        e = jnp.exp(-jnp.abs(x))
        coef = jnp.where(x >= 0, 1.0, e) / (1.0 + e)
        if positive is not None:
            coef = jnp.where(positive, -coef, coef)
        update = jnp.dot(coef.astype(jnp.bfloat16), others, preferred_element_type=jnp.float32)
        terms = fold(jnp.maximum(x, 0.0) + jnp.log1p(e)) if which == 0 else None
        if done[which]:
            hat[...] += update
            if which == 0:
                term_sum[...] += terms
        else:
            hat[...] = update
            if which == 0:
                term_sum[...] = terms
        done[which] = True

    def take_sibling(which, step, d):
        for part in range(2):
            take(which, step, 2 * lax.rem(c + d, chips) + 1 - k, part)

    for which in range(2):
        take_sibling(which, 0, 0)
        score(which, 0, 0)

    def arrive(which, part):
        for d in range(1, chips):
            take(which, 0, same_core(d), part)
            if part == 0:
                to_next(which, same_core(d), 0)
            to_sibling(which, 0, same_core(d), part)
        take(which, 1, m, 1 - part)
        if part == 0:
            to_peers(which, 1, m, 1)
        to_sibling(which, 1, m, 1 - part)

    def last(which):
        for d in range(1, chips):
            for part in range(2):
                take(which, 1, same_core(d), part)
                to_sibling(which, 1, same_core(d), part)

    def score_first(which):
        for d in range(1, chips):
            take_sibling(which, 0, d)
            score(which, 0, d)
        take_sibling(which, 1, 0)
        score(which, 1, 0)

    for part in range(2):
        sent(group_copies[part])
        sent(next_copies[part])
        start_both(made(to_peers, 1, 0, m, part), made(to_next, 1, m, 1 - part))
        arrive(0, part)
    arrive(1, 0)
    score_first(0)
    last(0)
    for d in range(1, chips):
        score(0, 1, d, k)
        take_sibling(0, 1, d)
        score(0, 1, d, 1 - k)

    group_terms[m] = term_sum[...]
    for d in range(1, n_mp):
        push(group_terms.at[m], group_terms.at[m], group_sem.at[m], (g, peer(d)))
    image_grad_ref[...] = back_norm(image_hat[...], image_ref[...])
    arrive(1, 1)
    for d in range(1, n_mp):
        await_copy(group_terms.at[peer(d)], group_sem.at[peer(d)])
    all_terms[g] = jnp.sum(group_terms[...], axis=0)
    for d in range(1, n_dp):
        push(all_terms.at[g], all_terms.at[g], all_sem.at[g], (ring(d), m))
    score_first(1)
    last(1)
    for d in range(1, chips):
        score(1, 1, d, k)
        take_sibling(1, 1, d)
        score(1, 1, d, 1 - k)
    text_grad_ref[...] = back_norm(text_hat[...], text_ref[...])
    for d in range(1, n_dp):
        await_copy(all_terms.at[ring(d)], all_sem.at[ring(d)])
    pair_count = n_dp * n_mp * rows * STEPS * n_mp * rows
    loss_ref[0] = jnp.sum(jnp.sum(all_terms[...], axis=0)) / pair_count
    for copy in sends:
        if not any(copy is other for other in waited):
            copy.wait_send()


def solution(mesh):
    n_dp, n_mp = mesh.shape["dp"], mesh.shape["mp"]

    def body(image_embed, text_embed, log_scale, logit_bias):
        rows, width = image_embed.shape
        chips = n_mp // 2
        others = chips - 1
        n_sends = 2 * (2 * others + 4) + 2 * (3 * others + 1) + 2 * (others + 1)
        n_sends += 2 * 2 * others + (n_mp - 1) + (n_dp - 1)
        vmem = pl.BlockSpec(memory_space=pltpu.VMEM)
        hbm = pl.BlockSpec(memory_space=pl.ANY)
        smem = pl.BlockSpec(memory_space=pltpu.SMEM)
        grad = jax.ShapeDtypeStruct((rows, width), jnp.float32)
        loss, image_grad, text_grad = pl.pallas_call(
            functools.partial(kernel, n_dp, n_mp),
            out_shape=(jax.ShapeDtypeStruct((1,), jnp.float32), grad, grad),
            in_specs=[hbm, hbm, smem, smem],
            out_specs=(smem, vmem, vmem),
            scratch_shapes=[
                pltpu.VMEM((rows, width), jnp.bfloat16),
                pltpu.VMEM((rows, width), jnp.bfloat16),
                pltpu.VMEM((2, n_mp * rows, width), jnp.bfloat16),
                pltpu.VMEM((2, n_mp * rows, width), jnp.bfloat16),
                pltpu.VMEM((rows, width), jnp.float32),
                pltpu.VMEM((rows, width), jnp.float32),
                pltpu.VMEM((8, 128), jnp.float32),
                pltpu.VMEM((n_mp, 8, 128), jnp.float32),
                pltpu.VMEM((n_dp, 8, 128), jnp.float32),
                pltpu.SemaphoreType.DMA((2,)),
                pltpu.SemaphoreType.DMA((n_sends,)),
                pltpu.SemaphoreType.DMA((2, 2, n_mp, 2)),
                pltpu.SemaphoreType.DMA((n_mp,)),
                pltpu.SemaphoreType.DMA((n_dp,)),
            ],
            compiler_params=pltpu.CompilerParams(
                collective_id=0, has_side_effects=True, vmem_limit_bytes=60 * 1024 * 1024
            ),
        )(image_embed, text_embed, log_scale, logit_bias)
        scale = jnp.exp(log_scale[0])
        return loss, scale * image_grad, scale * text_grad

    rows_spec = P(("dp", "mp"), None)
    return jax.shard_map(
        body,
        mesh=mesh,
        in_specs=(rows_spec, rows_spec, P(), P()),
        out_specs=(P(), rows_spec, rows_spec),
        check_vma=False,
    )
```

```python
import functools

import jax
import jax.numpy as jnp
from jax import lax
from jax.experimental import pallas as pl
from jax.experimental.pallas import tpu as pltpu
from jax.sharding import PartitionSpec as P

STEPS = 2
MESH = pl.DeviceIdType.MESH
NT = (((1,), (1,)), ((), ()))


def unit_rows(raw):
    values = raw.astype(jnp.float32)
    norm = jnp.sqrt(jnp.sum(values * values, axis=1, keepdims=True) + 1e-06)
    return (values / norm, norm)


def back_norm(hat, raw):
    unit, norm = unit_rows(raw)
    return (hat - unit * jnp.sum(unit * hat, axis=1, keepdims=True)) / norm


def fold(values):
    rows, columns = values.shape
    tall = values[0:8]
    for r in range(8, rows, 8):
        tall = tall + values[r : r + 8]
    tile = tall[:, 0:128]
    for c in range(128, columns, 128):
        tile = tile + tall[:, c : c + 128]
    return tile


def kernel(
    n_dp, n_mp, image_hbm, text_hbm, log_scale_ref, bias_ref,
    loss_ref, image_grad_ref, text_grad_ref,
    image_ref, text_ref, texts, images, image_hat, text_hat, term_sum, group_terms, all_terms,
    load_sem, send_sem, row_sem, group_sem, all_sem,
):
    rows = image_ref.shape[0]
    chips, cut = n_mp // 2, rows * 3 // 8
    g, m = lax.axis_index("dp"), lax.axis_index("mp")
    c, k = m // 2, lax.rem(m, 2)
    sibling = 2 * c + 1 - k
    towards = (lax.rem(g + 1, n_dp), lax.rem(g + n_dp - 1, n_dp))

    def same_core(d):
        return 2 * lax.rem(c + d, chips) + k

    def peer(d):
        return lax.rem(m + d, n_mp)

    def ring(d):
        return lax.rem(g + d, n_dp)

    loads = [
        pltpu.make_async_copy(text_hbm, text_ref, load_sem.at[0]),
        pltpu.make_async_copy(image_hbm, image_ref, load_sem.at[1]),
    ]
    for load in loads:
        load.start()

    partners = [(g, peer(d)) for d in range(1, n_mp)]
    partners += [(ring(d), m) for d in range(1, n_dp)]
    barrier = pltpu.get_barrier_semaphore()
    for partner in partners:
        pl.semaphore_signal(barrier, inc=1, device_id=partner, device_id_type=MESH)

    def block(which, step, index, part=None):
        ref = (texts, images)[which]
        if part is None:
            return ref.at[step, pl.ds(pl.multiple_of(index * rows, rows), rows), :]
        start = pl.multiple_of(index * rows + part * cut, 16)
        return ref.at[step, pl.ds(start, (cut, rows - cut)[part]), :]

    def normalise(which):
        loads[which].wait()
        low = unit_rows((text_ref, image_ref)[which][...])[0].astype(jnp.bfloat16)
        block(which, 0, m)[...] = low

    normalise(0)
    pl.semaphore_wait(barrier, len(partners))

    sends, held = [], []

    def push(src, dst, recv, device):
        copy = pltpu.make_async_remote_copy(
            src_ref=src, dst_ref=dst, send_sem=send_sem.at[len(sends)], recv_sem=recv,
            device_id=device, device_id_type=MESH,
        )
        sends.append(copy)
        if not held:
            copy.start()

    def await_copy(dst, recv):
        pltpu.make_async_remote_copy(
            src_ref=dst, dst_ref=dst, send_sem=send_sem.at[0], recv_sem=recv,
            device_id=(g, sibling), device_id_type=MESH,
        ).wait_recv()

    def send(which, step, index, part, device, to_step):
        push(block(which, step, index, part), block(which, to_step, index, part),
             row_sem.at[which, to_step, index, part], device)

    def take(which, step, index, part):
        await_copy(block(which, step, index, part), row_sem.at[which, step, index, part])

    def to_peers(which, step, index, part):
        for d in range(1, chips):
            send(which, step, index, part, (g, same_core(d)), step)

    def to_next(which, index, part):
        send(which, 0, index, part, (towards[which], m), 1)

    def to_sibling(which, step, index, part):
        send(which, step, index, part, (g, sibling), step)

    def made(step, *rest):
        held.append(True)
        first = len(sends)
        step(*rest)
        held.pop()
        return sends[first:]

    def start_both(one, two):
        for core, order in enumerate((one + two, two + one)):
            @pl.when(k == core)
            def _():
                for copy in order:
                    copy.start()

    def sent(copies):
        for copy in copies:
            copy.wait_send()
        waited.extend(copies)

    waited = []
    group_copies, next_copies = [], []
    for part in range(2):
        group_copies.append(made(to_peers, 0, 0, m, part))
        next_copies.append(made(to_next, 0, m, 1 - part))
        start_both(group_copies[part], next_copies[part])
    for part in range(2):
        to_sibling(0, 0, m, part)
    normalise(1)
    for part in range(2):
        to_sibling(1, 0, m, part)

    scale = jnp.exp(jnp.full((rows, 1), log_scale_ref[0], jnp.float32))
    bias = bias_ref[0]
    pair = 2 * rows
    done = [False, False]

    def score(which, step, d, core=None):
        low = block(1 - which, 0, m)
        hat = (image_hat, text_hat)[which]
        chip = lax.rem(c + d, chips)
        if core is None:
            others = (texts, images)[which][step, pl.ds(pl.multiple_of(chip * pair, pair), pair), :]
        else:
            others = block(which, step, 2 * chip + core)[...]
        z = scale * lax.dot_general(low[...], others, NT, preferred_element_type=jnp.float32) + bias
        positive = None
        x = z
        if step == 0 and d == 0:
            row = lax.broadcasted_iota(jnp.int32, (rows, pair), 0)
            column = lax.broadcasted_iota(jnp.int32, (rows, pair), 1)
            positive = row + k * rows == column
            x = jnp.where(positive, -z, z)
        e = jnp.exp(-jnp.abs(x))
        coef = jnp.where(x >= 0, 1.0, e) / (1.0 + e)
        if positive is not None:
            coef = jnp.where(positive, -coef, coef)
        update = jnp.dot(coef.astype(jnp.bfloat16), others, preferred_element_type=jnp.float32)
        terms = fold(jnp.maximum(x, 0.0) + jnp.log1p(e)) if which == 0 else None
        if done[which]:
            hat[...] += update
            if which == 0:
                term_sum[...] += terms
        else:
            hat[...] = update
            if which == 0:
                term_sum[...] = terms
        done[which] = True

    def take_sibling(which, step, d):
        for part in range(2):
            take(which, step, 2 * lax.rem(c + d, chips) + 1 - k, part)

    for which in range(2):
        take_sibling(which, 0, 0)
        score(which, 0, 0)

    def arrive(which, part):
        for d in range(1, chips):
            take(which, 0, same_core(d), part)
            if part == 0:
                to_next(which, same_core(d), 0)
            to_sibling(which, 0, same_core(d), part)
        take(which, 1, m, 1 - part)
        if part == 0:
            to_peers(which, 1, m, 1)
        to_sibling(which, 1, m, 1 - part)

    def last(which):
        for d in range(1, chips):
            for part in range(2):
                take(which, 1, same_core(d), part)
                to_sibling(which, 1, same_core(d), part)

    def score_first(which):
        for d in range(1, chips):
            take_sibling(which, 0, d)
            score(which, 0, d)
        take_sibling(which, 1, 0)
        score(which, 1, 0)

    for part in range(2):
        sent(group_copies[part])
        start_both(made(to_peers, 1, 0, m, part), made(to_next, 1, m, 1 - part))
        arrive(0, part)
    arrive(1, 0)
    score_first(0)
    last(0)
    for d in range(1, chips):
        score(0, 1, d, k)
        take_sibling(0, 1, d)
        score(0, 1, d, 1 - k)

    group_terms[m] = term_sum[...]
    for d in range(1, n_mp):
        push(group_terms.at[m], group_terms.at[m], group_sem.at[m], (g, peer(d)))
    image_grad_ref[...] = back_norm(image_hat[...], image_ref[...])
    arrive(1, 1)
    for d in range(1, n_mp):
        await_copy(group_terms.at[peer(d)], group_sem.at[peer(d)])
    all_terms[g] = jnp.sum(group_terms[...], axis=0)
    for d in range(1, n_dp):
        push(all_terms.at[g], all_terms.at[g], all_sem.at[g], (ring(d), m))
    score_first(1)
    last(1)
    for d in range(1, chips):
        score(1, 1, d, k)
        take_sibling(1, 1, d)
        score(1, 1, d, 1 - k)
    text_grad_ref[...] = back_norm(text_hat[...], text_ref[...])
    for d in range(1, n_dp):
        await_copy(all_terms.at[ring(d)], all_sem.at[ring(d)])
    pair_count = n_dp * n_mp * rows * STEPS * n_mp * rows
    loss_ref[0] = jnp.sum(jnp.sum(all_terms[...], axis=0)) / pair_count
    for copy in sends:
        if not any(copy is other for other in waited):
            copy.wait_send()


def solution(mesh):
    n_dp, n_mp = mesh.shape["dp"], mesh.shape["mp"]

    def body(image_embed, text_embed, log_scale, logit_bias):
        rows, width = image_embed.shape
        chips = n_mp // 2
        others = chips - 1
        n_sends = 2 * (2 * others + 4) + 2 * (3 * others + 1) + 2 * (others + 1)
        n_sends += 2 * 2 * others + (n_mp - 1) + (n_dp - 1)
        vmem = pl.BlockSpec(memory_space=pltpu.VMEM)
        hbm = pl.BlockSpec(memory_space=pl.ANY)
        smem = pl.BlockSpec(memory_space=pltpu.SMEM)
        grad = jax.ShapeDtypeStruct((rows, width), jnp.float32)
        loss, image_grad, text_grad = pl.pallas_call(
            functools.partial(kernel, n_dp, n_mp),
            out_shape=(jax.ShapeDtypeStruct((1,), jnp.float32), grad, grad),
            in_specs=[hbm, hbm, smem, smem],
            out_specs=(smem, vmem, vmem),
            scratch_shapes=[
                pltpu.VMEM((rows, width), jnp.bfloat16),
                pltpu.VMEM((rows, width), jnp.bfloat16),
                pltpu.VMEM((2, n_mp * rows, width), jnp.bfloat16),
                pltpu.VMEM((2, n_mp * rows, width), jnp.bfloat16),
                pltpu.VMEM((rows, width), jnp.float32),
                pltpu.VMEM((rows, width), jnp.float32),
                pltpu.VMEM((8, 128), jnp.float32),
                pltpu.VMEM((n_mp, 8, 128), jnp.float32),
                pltpu.VMEM((n_dp, 8, 128), jnp.float32),
                pltpu.SemaphoreType.DMA((2,)),
                pltpu.SemaphoreType.DMA((n_sends,)),
                pltpu.SemaphoreType.DMA((2, 2, n_mp, 2)),
                pltpu.SemaphoreType.DMA((n_mp,)),
                pltpu.SemaphoreType.DMA((n_dp,)),
            ],
            compiler_params=pltpu.CompilerParams(
                collective_id=0, has_side_effects=True, vmem_limit_bytes=60 * 1024 * 1024
            ),
        )(image_embed, text_embed, log_scale, logit_bias)
        scale = jnp.exp(log_scale[0])
        return loss, scale * image_grad, scale * text_grad

    rows_spec = P(("dp", "mp"), None)
    return jax.shard_map(
        body,
        mesh=mesh,
        in_specs=(rows_spec, rows_spec, P(), P()),
        out_specs=(P(), rows_spec, rows_spec),
        check_vma=False,
    )
```
